128 devices in a mesh: row: 8 (over z, x_lo), col: 16 (over x_hi, y, core).
Axes of the slice: x: 4 (x_hi: 2, x_lo: 2; x = x_hi * 2 + x_lo), y: 4, z: 4, core: 2. Of those that a mesh axis runs over, the one named last changes fastest.
Arguments:
- front: float32 [45056, 4096], P('row', 'col'), may hold values from -6 to 278, as said below
- children: float32 [32768, 4096], P('row', 'col'), may hold values from -6 to 6
- row_map: int32 [256], replicated, may hold values from 0 to 351, as said below
- col_map: int32 [64], replicated, may hold values from 0 to 31, as said below
Outputs:
- updated: float32 [45056, 4096], P('row', 'col')
The draws below stay inside these ranges and needn't reach their ends.
Inputs may be any that keep to these rules, and one draw needn't show every extreme that they name: `front`: the symmetric part of the assembled leading 512 x 512 block is positive definite. `row_map`: within one child no front row block is named twice. Of the 32 child row blocks stored on one device, at most 8 name front row blocks of one owner (block index modulo 8); one owner, the same for every device, is named exactly 8 times by every device. Within one child no front column block is named twice, and col_map[h * 32 + b] modulo 16 equals b // 2.
All inputs are finite; a program needn't handle non-finite values.
Results may differ from the reference program's by a relative error of at most 0.00005.
Values sent between devices are 32-bit elements; how exact they have to be, the bound alone decides.
A program may use at most 128 MiB of HBM per device.

```python
import jax
import jax.numpy as jnp
from jax import lax

BLK = 128
NF = 45056
SLAB = 4096
PANEL = 512
CBR_DEV = 32
CBC_DEV = 2
KR = 44
KC = 2
MOST = 8
CBR = 128
CBC = 32
CR = 16384
CC = 4096
N_ROW = 8
N_COL = 16


def natural_index(position, per_device, device_count):
    device = position // (per_device * BLK)
    within = position % (per_device * BLK)
    return (within // BLK * device_count + device) * BLK + position % BLK


def draw_front(key, part):
    row_devices = NF // (BLK * KR)
    col_devices = SLAB // (BLK * KC)
    row_index = natural_index(jnp.arange(NF), KR, row_devices)
    col_index = natural_index(jnp.arange(SLAB), KC, col_devices)
    first_key = jax.random.fold_in(key, 0)
    values = jax.random.truncated_normal(first_key, -6.0, 6.0, (NF, SLAB), jnp.float32)
    shift = float(PANEL // 2 + 16)
    return values + jnp.where(row_index[:, None] == col_index[None, :], shift, 0.0)


def draw_row_map(key, part):
    row_devices = 2 * CBR // CBR_DEV
    halfway = row_devices // 2
    common = jax.random.randint(jax.random.fold_in(key, 5), (), 0, row_devices)
    counter = jnp.arange(CBR_DEV)

    def one_source(source_key):
        order_key, spare_key, shuffle_key = jax.random.split(source_key, 3)
        others = (common + 1 + jax.random.permutation(order_key, row_devices - 1)) % row_devices
        spare = jax.random.permutation(spare_key, (row_devices - 1) * MOST)[:CBR_DEV - MOST]
        owners = jnp.concatenate([jnp.zeros((MOST,), jnp.int32) + common, others[spare // MOST]])
        earlier = (owners[:, None] == owners[None, :]) & (counter[None, :] < counter[:, None])
        ranks = jnp.sum(earlier.astype(jnp.int32), axis=1)
        shuffle = jax.random.permutation(shuffle_key, CBR_DEV)
        return (owners[shuffle], ranks[shuffle])

    def one_child(child_key):
        source_keys = jax.random.split(jax.random.fold_in(child_key, 1), halfway)
        owners, ranks = jax.vmap(one_source)(source_keys)
        place_keys = jax.random.split(jax.random.fold_in(child_key, 2), row_devices)
        places = jax.vmap(lambda place_key: jax.random.permutation(place_key, KR))(place_keys)
        position = jnp.arange(halfway)[:, None] * MOST + ranks
        local = places[owners, position]
        return (local * row_devices + owners).reshape(-1)
    first = one_child(jax.random.fold_in(key, 10))
    second = one_child(jax.random.fold_in(key, 11))
    return jnp.concatenate([first, second]).astype(jnp.int32)


def draw_col_map(key, part):
    col_devices = CBC // CBC_DEV
    device_keys = jax.random.split(key, 2 * col_devices)
    locals_drawn = jax.vmap(lambda device_key: jax.random.permutation(device_key, KC)[:CBC_DEV])(device_keys)
    locals_drawn = locals_drawn.reshape(2, col_devices, CBC_DEV)
    return (locals_drawn * col_devices + jnp.arange(col_devices)[None, :, None]).reshape(-1).astype(jnp.int32)


def level_of(stream_key, shape, cuts, smallest, largest):
    factor_of = 1.0
    for dim, blocks in cuts:
        heights = jax.random.uniform(jax.random.fold_in(jax.random.fold_in(stream_key, 6), dim), (blocks,), jnp.float32, smallest / len(cuts), largest / len(cuts))
        factor_of = factor_of * jnp.repeat(jnp.exp(heights), shape[dim] // blocks).reshape((-1,) + (1,) * (len(shape) - 1 - dim))
    return factor_of


def scatter_about(key, extent, width, reach, cuts=(), held_as=jnp.bfloat16):
    values = width * jax.random.normal(key, extent, jnp.float32)
    if cuts:
        values = values * level_of(key, extent, cuts, -0.22, 0.18)
    return jnp.clip(values, -reach, reach).astype(held_as)


def setup_inputs(seed: int = 0) -> dict:
    key_of = jax.random.split(jax.random.key(seed), 5)
    front = draw_front(jax.random.fold_in(key_of[4], 71), 0)
    children = scatter_about(key_of[1], (2 * CR, CC), 1.0, 6.0, ((0, 8), (1, 16)), jnp.float32)
    row_map = draw_row_map(jax.random.fold_in(key_of[4], 71), 0)
    col_map = draw_col_map(jax.random.fold_in(key_of[4], 71), 0)
    return {"front": front, "children": children, "row_map": row_map, "col_map": col_map}


def reference(front, children, row_map, col_map):
    natural = front.reshape(N_ROW, KR, BLK, N_COL, KC, BLK).transpose(1, 0, 2, 4, 3, 5)
    blocks = natural.reshape(KR * N_ROW, BLK, KC * N_COL, BLK)
    for child in range(2):
        child_tiles = children[child * CR:(child + 1) * CR].reshape(CBR, BLK, CBC, BLK).transpose(0, 2, 1, 3)
        row_blocks = row_map[child * CBR:(child + 1) * CBR]
        col_blocks = col_map[child * CBC:(child + 1) * CBC]
        blocks = blocks.at[row_blocks[:, None], :, col_blocks[None, :], :].add(child_tiles)
    assembled = blocks.reshape(NF, SLAB)
    leading = assembled[:PANEL, :PANEL]
    lower_factor = jnp.linalg.cholesky((leading + leading.T) * 0.5)
    factor = jax.scipy.linalg.solve_triangular(lower_factor, assembled[:, :PANEL].T, lower=True).T
    factor = jnp.concatenate([lower_factor, factor[PANEL:]], axis=0)
    trailing = assembled - jnp.dot(factor, factor[:SLAB].T, precision=lax.Precision.HIGHEST)
    trailing = jnp.concatenate([factor, trailing[:, PANEL:]], axis=1)
    stored = trailing.reshape(KR, N_ROW, BLK, KC, N_COL, BLK).transpose(1, 0, 2, 4, 3, 5)
    return stored.reshape(NF, SLAB)
```

```python
import jax
import jax.numpy as jnp
from jax import lax
from jax.experimental import pallas as pl
from jax.experimental.pallas import tpu as pltpu
from jax.sharding import PartitionSpec as P

BLK = 128
PANEL = 512
NR = 8
NC = 16
MOST = 8
SLOTS = NR * MOST
KR = 44
CHUNK = 4 * BLK
NCH = KR * BLK // CHUNK
HI = lax.Precision.HIGHEST
MESH = pl.DeviceIdType.MESH
F32 = jnp.float32
BF16 = jnp.bfloat16


def nt(a, b, precision=None):
    return lax.dot_general(
        a, b, (((1,), (1,)), ((), ())), precision=precision, preferred_element_type=F32
    )


def nn(a, b, precision=None):
    return lax.dot_general(
        a, b, (((1,), (0,)), ((), ())), precision=precision, preferred_element_type=F32
    )


def split(x):
    high = x.astype(BF16)
    return high, (x - high.astype(F32)).astype(BF16)


def inverse_of_factor(a):
    rows = lax.broadcasted_iota(jnp.int32, (BLK, 1), 0)
    eye = rows == lax.broadcasted_iota(jnp.int32, (BLK, BLK), 1)
    e = eye.astype(F32)
    done_a, done_e = [], []
    for first in range(0, BLK, 32):
        below = rows[first:]
        for j in range(first, first + 32):
            i = j - first
            pivot = 1.0 / a[i : i + 1, j : j + 1]
            col = jnp.where(below > j, a[:, j : j + 1], 0.0)
            row_a = a[i : i + 1, :] * pivot
            row_e = e[i : i + 1, :] * pivot
            a = a - col * row_a
            e = e - col * row_e
        done_a.append(a[:32])
        done_e.append(e[:32])
        a, e = a[32:], e[32:]
    a = jnp.concatenate(done_a, axis=0)
    e = jnp.concatenate(done_e, axis=0)
    d = jnp.sum(jnp.where(eye, a, 0.0), axis=1, keepdims=True)
    s = lax.rsqrt(d)
    s = s * (1.5 - 0.5 * d * s * s)
    return e * s


def kernel(
    tbl, front, children, out,
    stage0, stage1, in0, in1, panel, sbuf, psbuf, smat, xmat, wth, wtl,
    ex_send, ex_recv, own_sem, bc_send, bc_recv, s_send, s_recv, p_send, p_recv,
):
    r = lax.axis_index("row")
    c = lax.axis_index("col")
    x_hi = c // 8
    y = (c // 2) % 4
    core = c % 2
    is_panel = c < 4
    stages = (stage0, stage1)
    ins = (in0, in1)

    barrier = pltpu.get_barrier_semaphore()

    @pl.loop(1, NR)
    def _(i):
        pl.semaphore_signal(barrier, inc=1, device_id={"row": (r + i) % NR}, device_id_type=MESH)

    @pl.loop(1, NC)
    def _(i):
        pl.semaphore_signal(barrier, inc=1, device_id={"col": (c + i) % NC}, device_id_type=MESH)

    swap = tbl[SLOTS + 2 * KR] == 1

    def ex_copy(q, i):
        to = (r + i) % NR
        return pltpu.make_async_remote_copy(
            src_ref=stages[q].at[pl.ds(to * MOST, MOST)],
            dst_ref=ins[q].at[pl.ds(r * MOST, MOST)],
            send_sem=ex_send.at[q * NR + i],
            recv_sem=ex_recv.at[q * NR + i],
            device_id={"row": to},
            device_id_type=MESH,
        )

    def own_copy(q):
        return pltpu.make_async_copy(
            stages[q].at[pl.ds(r * MOST, MOST)], ins[q].at[pl.ds(r * MOST, MOST)], own_sem.at[q]
        )

    def fill(q, to):
        @pl.loop(0, MOST)
        def _(j):
            slot = to * MOST + j
            block = children[tbl[slot]]
            left, right = block[:, :BLK], block[:, BLK:]
            if q == 0:
                stages[q][slot] = jnp.where(swap, right, left)
            else:
                stages[q][slot] = jnp.where(swap, left, right)

    def assemble(q):
        cols = slice(q * BLK, (q + 1) * BLK)

        @pl.loop(0, KR)
        def _(k):
            at = pl.ds(pl.multiple_of(k * BLK, BLK), BLK)
            total = (
                front[at, cols] + ins[q][tbl[SLOTS + k]] + ins[q][tbl[SLOTS + KR + k]]
            )
            out[at, cols] = total
            if q == 0:

                @pl.when(is_panel)
                def _():
                    panel[c, at, :] = total

    fill(0, (r + 1) % NR)
    pl.semaphore_wait(barrier, NR - 1 + NC - 1)
    ex_copy(0, 1).start()

    @pl.loop(2, NR)
    def _(i):
        fill(0, (r + i) % NR)
        ex_copy(0, i).start()

    fill(0, r)
    own_copy(0).start()
    for q in range(2):
        ins[q][SLOTS] = jnp.zeros((BLK, BLK), F32)

    @pl.loop(0, NR)
    def _(i):
        fill(1, i)

    xmat[...] = jnp.zeros_like(xmat)
    own_copy(0).wait()

    @pl.loop(1, NR)
    def _(i):
        ex_copy(0, i).wait_recv()

    assemble(0)

    def bc_copy(s, i, d, to):
        at = pl.ds(pl.multiple_of(i * CHUNK, CHUNK), CHUNK)
        return pltpu.make_async_remote_copy(
            src_ref=panel.at[s, at],
            dst_ref=panel.at[s, at],
            send_sem=bc_send.at[(s * 4 + d) * NCH + i],
            recv_sem=bc_recv.at[s * NCH + i],
            device_id={"col": to},
            device_id_type=MESH,
        )

    def targets(g, i):
        yp = y if g == 0 else (5 - y) % 4
        even = i % 2 == 0
        odd = i % 2 == 1
        up, down = (yp + 1) % 4, (yp + 3) % 4
        y_up = up if g == 0 else (5 - up) % 4
        y_down = down if g == 0 else (5 - down) % 4
        here, there = x_hi == 0, x_hi == 1
        return (
            (
                (here & (yp == 0)) | (there & ((even & (yp == 0)) | (odd & (yp == 3)))),
                x_hi * 8 + y_up * 2 + core,
            ),
            (
                (yp == 3) | ((yp == 0) & (here | even)) | (there & odd & (yp == 2)),
                x_hi * 8 + y_down * 2 + core,
            ),
            (
                here & ((even & (yp == 0)) | (odd & (yp == 3))),
                8 + y * 2 + core,
            ),
            (core >= 0, x_hi * 8 + y * 2 + 1 - core),
        )

    def forward(i):
        for g in range(2):
            s = 2 * g + core

            @pl.when(c != s)
            def _():
                bc_copy(s, i, 0, c).wait_recv()

            for d, (when, to) in enumerate(targets(g, i)):

                @pl.when(when)
                def _():
                    bc_copy(s, i, d, to).start()

    def from_sibling(i):
        for g in range(2):
            s = 2 * g + 1 - core
            bc_copy(s, i, 0, c).wait_recv()

    forward(0)
    from_sibling(0)

    def s_copy(i):
        return pltpu.make_async_remote_copy(
            src_ref=panel.at[:, pl.ds(0, BLK)],
            dst_ref=sbuf.at[r],
            send_sem=s_send.at[i],
            recv_sem=s_recv.at[r],
            device_id={"row": (r + i) % NR},
            device_id_type=MESH,
        )

    def s_wait(source):
        pltpu.make_async_remote_copy(
            src_ref=panel.at[:, pl.ds(0, BLK)],
            dst_ref=sbuf.at[source],
            send_sem=s_send.at[0],
            recv_sem=s_recv.at[source],
            device_id={"row": r},
            device_id_type=MESH,
        ).wait_recv()

    def p_copy(i, k):
        at = pl.ds(pl.multiple_of((x_hi + 2 * k) * BLK, BLK), BLK)
        return pltpu.make_async_remote_copy(
            src_ref=panel.at[:, at],
            dst_ref=psbuf.at[k],
            send_sem=p_send.at[k * NR + i],
            recv_sem=p_recv.at[k],
            device_id={"row": (r + i) % NR},
            device_id_type=MESH,
        )

    is_lead = r < 4
    is_root = r == c % NR

    @pl.when(is_lead)
    def _():
        @pl.loop(1, NR)
        def _(i):
            s_copy(i).start()

        sbuf[r] = panel[:, pl.ds(0, BLK), :]

    @pl.when(is_root)
    def _():
        @pl.loop(1, NR)
        def _(i):
            for k in range(2):
                p_copy(i, k).start()

        for k in range(2):
            at = pl.ds(pl.multiple_of((x_hi + 2 * k) * BLK, BLK), BLK)
            psbuf[k] = panel[:, at, :]

    forward(1)
    forward(2)

    @pl.loop(0, 4)
    def _(source):
        @pl.when(source != r)
        def _():
            s_wait(source)

    @pl.loop(1, NR)
    def _(i):
        ex_copy(1, i).start()

    own_copy(1).start()

    for i in range(4):
        for j in range(4):
            smat[i * BLK : (i + 1) * BLK, j * BLK : (j + 1) * BLK] = 0.5 * (
                sbuf[i, j] + sbuf[j, i].T
            )

    @pl.loop(0, 4)
    def _(b):
        at = pl.ds(pl.multiple_of(b * BLK, BLK), BLK)
        x = xmat[...]
        lb = nt(smat[at, :], x, HI)
        block = smat[at, at] - nt(lb, lb, HI)
        v = inverse_of_factor(block)
        xmat[at, :] = -nn(v, nn(lb, x, HI), HI)
        xmat[at, at] = v
        forward(2 * b + 3)
        forward(2 * b + 4)

    @pl.when(jnp.logical_not(is_root))
    def _():
        for k in range(2):
            p_copy(0, k).wait_recv()

    for k in range(2):
        ps = jnp.concatenate([psbuf[k, s] for s in range(4)], axis=1)
        wt = nn(nt(ps, xmat[...], HI), xmat[...], HI)
        if k == 0:
            at = pl.ds(pl.multiple_of((c % 4) * BLK, BLK), BLK)
            wt = jnp.where(is_panel, -xmat[at, :], wt)
        high, low = split(wt)
        wth[k * BLK : (k + 1) * BLK, :] = high
        wtl[k * BLK : (k + 1) * BLK, :] = low

    own_copy(1).wait()

    @pl.loop(1, NR)
    def _(i):
        ex_copy(1, i).wait_recv()

    assemble(1)

    keep = jnp.where(
        is_panel & (lax.broadcasted_iota(jnp.int32, (1, 2 * BLK), 1) < BLK), 0.0, 1.0
    ).astype(F32)

    @pl.loop(1, NCH)
    def _(i):
        from_sibling(i)

    @pl.when(is_lead)
    def _():
        at = pl.ds(pl.multiple_of((r % 4) * BLK, BLK), BLK)
        for s in range(4):
            sbuf[0, s] = smat[at, s * BLK : (s + 1) * BLK]

    @pl.when(jnp.logical_not(is_lead))
    def _():
        for s in range(4):
            sbuf[0, s] = panel[s, 0:BLK, :]

    def update(parts, at):
        rows = jnp.concatenate(parts, axis=1)
        high, low = split(rows)
        total = nt(high, wth[...]) + (nt(high, wtl[...]) + nt(low, wth[...]))
        out[at, :] = out[at, :] * keep - total

    update([sbuf[0, s] for s in range(4)], pl.ds(0, BLK))
    update([panel[s, BLK : 2 * BLK, :] for s in range(4)], pl.ds(BLK, BLK))

    @pl.loop(1, KR // 2)
    def _(k):
        at = pl.ds(pl.multiple_of(k * 2 * BLK, 2 * BLK), 2 * BLK)
        update([panel[s, at, :] for s in range(4)], at)

    @pl.loop(1, NR)
    def _(i):
        for q in range(2):
            ex_copy(q, i).wait_send()

    @pl.when(is_lead)
    def _():
        @pl.loop(1, NR)
        def _(i):
            s_copy(i).wait_send()

    @pl.when(is_root)
    def _():
        @pl.loop(1, NR)
        def _(i):
            for k in range(2):
                p_copy(i, k).wait_send()

    @pl.loop(0, NCH)
    def _(i):
        for g in range(2):
            for d, (when, to) in enumerate(targets(g, i)):

                @pl.when(when)
                def _():
                    bc_copy(2 * g + core, i, d, to).wait_send()


def tables(row_map, col_map):
    my_row = lax.axis_index("row")
    my_col = lax.axis_index("col")
    layout = row_map.reshape(NR, -1)
    count = layout.shape[1]
    owner = layout % NR
    counter = jnp.arange(count)
    earlier = (owner[:, :, None] == owner[:, None, :]) & (
        counter[None, None, :] < counter[None, :, None]
    )
    rank = jnp.sum(earlier.astype(jnp.int32), axis=2)
    slot_out = owner * MOST + rank
    mine = lax.dynamic_index_in_dim(slot_out, my_row, 0, keepdims=False)
    send = jnp.sum(
        jnp.where(mine[None, :] == jnp.arange(SLOTS)[:, None], counter[None, :], 0), axis=1
    )
    slot_in = (jnp.arange(NR)[:, None] * MOST + rank).reshape(2, -1)
    wanted = jnp.arange(KR) * NR + my_row
    hit = layout.reshape(2, 1, -1) == wanted[None, :, None]
    receive = SLOTS + jnp.sum(jnp.where(hit, slot_in[:, None, :] - SLOTS, 0), axis=2)
    child = my_row // (NR // 2)
    first = lax.dynamic_index_in_dim(
        col_map.reshape(2, NC, 2)[:, :, 0].reshape(-1), child * NC + my_col, 0
    )
    return jnp.concatenate([send, receive.reshape(-1), first // NC]).astype(jnp.int32)


def local(front, children, row_map, col_map):
    table = tables(row_map, col_map)
    vmem = pl.BlockSpec(memory_space=pltpu.VMEM)
    rows = front.shape[0]
    blocks = children.reshape(-1, BLK, 2 * BLK)
    tile = (BLK, BLK)
    return pl.pallas_call(
        kernel,
        out_shape=jax.ShapeDtypeStruct(front.shape, F32),
        in_specs=[pl.BlockSpec(memory_space=pltpu.SMEM), vmem, vmem],
        out_specs=vmem,
        scratch_shapes=[
            pltpu.VMEM((SLOTS,) + tile, F32),
            pltpu.VMEM((SLOTS,) + tile, F32),
            pltpu.VMEM((SLOTS + 1,) + tile, F32),
            pltpu.VMEM((SLOTS + 1,) + tile, F32),
            pltpu.VMEM((4, rows, BLK), F32),
            pltpu.VMEM((4, 4) + tile, F32),
            pltpu.VMEM((2, 4) + tile, F32),
            pltpu.VMEM((PANEL, PANEL), F32),
            pltpu.VMEM((PANEL, PANEL), F32),
            pltpu.VMEM((2 * BLK, PANEL), BF16),
            pltpu.VMEM((2 * BLK, PANEL), BF16),
            pltpu.SemaphoreType.DMA((2 * NR,)),
            pltpu.SemaphoreType.DMA((2 * NR,)),
            pltpu.SemaphoreType.DMA((2,)),
            pltpu.SemaphoreType.DMA((16 * NCH,)),
            pltpu.SemaphoreType.DMA((4 * NCH,)),
            pltpu.SemaphoreType.DMA((NR,)),
            pltpu.SemaphoreType.DMA((4,)),
            pltpu.SemaphoreType.DMA((2 * NR,)),
            pltpu.SemaphoreType.DMA((2,)),
        ],
        compiler_params=pltpu.CompilerParams(
            collective_id=0, has_side_effects=True, vmem_limit_bytes=60 * 2**20
        ),
    )(table, front, blocks)


def solution(mesh):
    placed = (P("row", "col"), P("row", "col"), P(), P())
    return jax.shard_map(
        local, mesh=mesh, in_specs=placed, out_specs=P("row", "col"), check_vma=False
    )
```

```python
import jax
import jax.numpy as jnp
from jax import lax
from jax.experimental import pallas as pl
from jax.experimental.pallas import tpu as pltpu
from jax.sharding import PartitionSpec as P

BLK = 128
PANEL = 512
NR = 8
NC = 16
MOST = 8
SLOTS = NR * MOST
KR = 44
SUB = 4
PART = BLK // SUB
SPAN = KR * PART
NCH = (PANEL + KR * BLK) // BLK
LEAD = PANEL // BLK
TURN = SPAN // BLK
UNIT = 11
WINDOW = 6
LAG = 4
STEPS = NCH + 4 * LAG
AHEAD = LEAD + 2 * TURN
HI = lax.Precision.HIGHEST
MESH = pl.DeviceIdType.MESH
F32 = jnp.float32
BF16 = jnp.bfloat16


def nt(a, b, precision=None):
    return lax.dot_general(
        a, b, (((1,), (1,)), ((), ())), precision=precision, preferred_element_type=F32
    )


def nn(a, b, precision=None):
    return lax.dot_general(
        a, b, (((1,), (0,)), ((), ())), precision=precision, preferred_element_type=F32
    )


def split(x):
    high = x.astype(BF16)
    return high, (x - high.astype(F32)).astype(BF16)


def inverse_of_factor(a, between):
    rows = lax.broadcasted_iota(jnp.int32, (BLK, 1), 0)
    eye = rows == lax.broadcasted_iota(jnp.int32, (BLK, BLK), 1)
    e = eye.astype(F32)
    done_a, done_e = [], []
    for first in range(0, BLK, 32):
        below = rows[first:]
        for j in range(first, first + 32):
            i = j - first
            pivot = 1.0 / a[i : i + 1, j : j + 1]
            col = jnp.where(below > j, a[:, j : j + 1], 0.0)
            row_a = a[i : i + 1, :] * pivot
            row_e = e[i : i + 1, :] * pivot
            a = a - col * row_a
            e = e - col * row_e
        done_a.append(a[:32])
        done_e.append(e[:32])
        a, e = a[32:], e[32:]
        between(first // 32)
    a = jnp.concatenate(done_a, axis=0)
    e = jnp.concatenate(done_e, axis=0)
    d = jnp.sum(jnp.where(eye, a, 0.0), axis=1, keepdims=True)
    s = lax.rsqrt(d)
    s = s * (1.5 - 0.5 * d * s * s)
    return e * s


def kernel(
    tbl, front, children_hbm, out,
    children, acc, stage0, stage1, in00, in01, in02, in03, in10, in11, in12, in13, stage_s, in_s, panel, psbuf, smat, xmat, block, lbx, wth, wtl,
    load_sem, ex_send, ex_recv, own_sem, bc_send, bc_recv, se_send, se_recv, s_send, s_recv, p_send, p_recv, out_sem,
):
    r = lax.axis_index("row")
    c = lax.axis_index("col")
    x_hi = c // 8
    y = (c // 2) % 4
    core = c % 2
    is_panel = c < 4
    is_lead = r < 4
    is_root = r == c % NR
    ins = (in00, in01, in02, in03, in10, in11, in12, in13)

    load_children = pltpu.make_async_copy(children_hbm, children, load_sem.at[0])
    load_front = pltpu.make_async_copy(front, acc, load_sem.at[1])
    load_children.start()
    load_front.start()

    barrier = pltpu.get_barrier_semaphore()

    @pl.loop(1, NR)
    def _(i):
        pl.semaphore_signal(barrier, inc=1, device_id={"row": (r + i) % NR}, device_id_type=MESH)

    @pl.loop(1, NC)
    def _(i):
        pl.semaphore_signal(barrier, inc=1, device_id={"col": (c + i) % NC}, device_id_type=MESH)

    swap = tbl[SLOTS + 2 * KR] == 1

    def ex_parts(t, slots):
        at = pl.ds(t % SUB * PART, PART)
        return (stage0 if t < SUB else stage1).at[slots, at]

    def ex_copy(t, i):
        to = (r + i) % NR
        return pltpu.make_async_remote_copy(
            src_ref=ex_parts(t, pl.ds(to * MOST, MOST)),
            dst_ref=ins[t].at[pl.ds(r * MOST, MOST)],
            send_sem=ex_send.at[t * NR + i],
            recv_sem=ex_recv.at[t * NR + i],
            device_id={"row": to},
            device_id_type=MESH,
        )

    def own_copy(t):
        mine = pl.ds(r * MOST, MOST)
        return pltpu.make_async_copy(ex_parts(t, mine), ins[t].at[mine], own_sem.at[t])

    def send_part(t):
        own_copy(t).start()

        @pl.loop(1, NR)
        def _(i):
            ex_copy(t, i).start()

    def sent_part(t):
        @pl.loop(1, NR)
        def _(i):
            ex_copy(t, i).wait_send()

    def got_part(t):
        own_copy(t).wait()

        @pl.loop(1, NR)
        def _(i):
            ex_copy(t, i).wait_recv()

    def se_copy(d):
        return pltpu.make_async_remote_copy(
            src_ref=stage_s.at[d],
            dst_ref=in_s.at[r],
            send_sem=se_send.at[d],
            recv_sem=se_recv.at[r],
            device_id={"row": d},
            device_id_type=MESH,
        )

    def se_wait(source):
        pltpu.make_async_remote_copy(
            src_ref=stage_s.at[0],
            dst_ref=in_s.at[source],
            send_sem=se_send.at[0],
            recv_sem=se_recv.at[source],
            device_id={"row": r},
            device_id_type=MESH,
        ).wait_recv()

    load_children.wait()

    @pl.loop(0, LEAD)
    def _(d):
        found = tbl[SLOTS + 2 * KR + 1 + d]
        block = children[jnp.maximum(found - 1, 0)]
        half = jnp.where(swap, block[:, BLK:], block[:, :BLK])
        stage_s[d] = jnp.where(found > 0, half, 0.0)

    pl.semaphore_wait(barrier, NR - 1 + NC - 1)

    @pl.when(is_panel)
    def _():
        @pl.loop(0, LEAD)
        def _(d):
            @pl.when(d != r)
            def _():
                se_copy(d).start()

    @pl.loop(0, SLOTS)
    def _(slot):
        block = children[tbl[slot]]
        stage0[slot] = jnp.where(swap, block[:, BLK:], block[:, :BLK])

    send_part(0)
    for t in range(2 * SUB):
        ins[t][SLOTS] = jnp.zeros((PART, BLK), F32)

    @pl.loop(0, SLOTS)
    def _(slot):
        block = children[tbl[slot]]
        stage1[slot] = jnp.where(swap, block[:, :BLK], block[:, BLK:])

    xmat[...] = jnp.zeros_like(xmat)
    load_front.wait()

    def s_copy(i):
        at = pl.ds(pl.multiple_of(r * BLK, BLK), BLK)
        return pltpu.make_async_remote_copy(
            src_ref=panel.at[c, at],
            dst_ref=panel.at[c, at],
            send_sem=s_send.at[i],
            recv_sem=s_recv.at[r],
            device_id={"row": (r + i) % NR},
            device_id_type=MESH,
        )

    def s_wait(source):
        at = pl.ds(pl.multiple_of(source * BLK, BLK), BLK)
        pltpu.make_async_remote_copy(
            src_ref=panel.at[c, at],
            dst_ref=panel.at[c, at],
            send_sem=s_send.at[0],
            recv_sem=s_recv.at[source],
            device_id={"row": r},
            device_id_type=MESH,
        ).wait_recv()

    @pl.when(is_panel & is_lead)
    def _():
        in_s[r] = stage_s[r]

        @pl.loop(0, NR)
        def _(source):
            @pl.when(source != r)
            def _():
                se_wait(source)

        total = acc[0, :, :BLK]
        for source in range(NR):
            total = total + in_s[source]
        panel[c, pl.ds(pl.multiple_of(r * BLK, BLK), BLK), :] = total

        @pl.loop(1, NR)
        def _(i):
            s_copy(i).start()

    @pl.when(is_panel)
    def _():
        @pl.loop(0, LEAD)
        def _(source):
            @pl.when(source != r)
            def _():
                s_wait(source)

    def bc_copy(s, i, d, to):
        at = pl.ds(pl.multiple_of(i * BLK, BLK), BLK)
        return pltpu.make_async_remote_copy(
            src_ref=panel.at[s, at],
            dst_ref=panel.at[s, at],
            send_sem=bc_send.at[(s * 4 + d) * NCH + i],
            recv_sem=bc_recv.at[s * NCH + i],
            device_id={"col": to},
            device_id_type=MESH,
        )

    def targets(g, i):
        yp = y if g == 0 else (5 - y) % 4
        even = i % 2 == 0
        odd = i % 2 == 1
        up, down = (yp + 1) % 4, (yp + 3) % 4
        y_up = up if g == 0 else (5 - up) % 4
        y_down = down if g == 0 else (5 - down) % 4
        here, there = x_hi == 0, x_hi == 1
        return (
            (
                (here & (yp == 0)) | (there & ((even & (yp == 0)) | (odd & (yp == 3)))),
                x_hi * 8 + y_up * 2 + core,
            ),
            (
                (yp == 3) | ((yp == 0) & (here | even)) | (there & odd & (yp == 2)),
                x_hi * 8 + y_down * 2 + core,
            ),
            (
                here & ((even & (yp == 0)) | (odd & (yp == 3))),
                8 + y * 2 + core,
            ),
            (core >= 0, x_hi * 8 + y * 2 + 1 - core),
        )

    def sent(g, i):
        for d, (when, to) in enumerate(targets(g, i)):

            @pl.when(when)
            def _():
                bc_copy(2 * g + core, i, d, to).wait_send()

    def forward(step):
        odd = step % 2
        for g in range(2):
            s = 2 * g + core
            yp = y if g == 0 else (5 - y) % 4
            near = jnp.where(yp == 0, 0, jnp.where(yp == 2, 2, 1))
            far_odd = jnp.where(yp == 3, 2, jnp.where(yp == 1, 4, 3))
            far = jnp.where(odd == 1, far_odd, near + 1)
            i = step - LAG * jnp.where(x_hi == 0, near, far)

            @pl.when((i >= 0) & (i < NCH))
            def _():
                @pl.when(c != s)
                def _():
                    bc_copy(s, i, 0, c).wait_recv()

                @pl.when((c == s) & (i >= WINDOW))
                def _():
                    sent(g, i - WINDOW)

                for d, (when, to) in enumerate(targets(g, i)):

                    @pl.when(when)
                    def _():
                        bc_copy(s, i, d, to).start()

    def from_sibling(i):
        for g in range(2):
            s = 2 * g + 1 - core
            bc_copy(s, i, 0, c).wait_recv()

    def forward_all(first, last):
        @pl.loop(first, last)
        def _(step):
            forward(step)

    def assemble(t, store):
        q, part = t // SUB, pl.ds(t % SUB * PART, PART)

        @pl.loop(0, KR)
        def _(k):
            total = (
                acc[k, part, q * BLK : (q + 1) * BLK]
                + ins[t][tbl[SLOTS + k]]
                + ins[t][tbl[SLOTS + KR + k]]
            )
            store(k, total)

    def assemble_here(t):
        q, part = t // SUB, pl.ds(t % SUB * PART, PART)

        def store(k, total):
            acc[k, part, q * BLK : (q + 1) * BLK] = total

        assemble(t, store)

    def phase(t):
        if t == 0:
            sent_part(0)
        if t < SUB - 1:
            send_part(t + 1)
        got_part(t)

        def store(k, total):
            at = pl.ds(pl.multiple_of(PANEL + t * SPAN + k * PART, PART), PART)
            panel[c, at, :] = total

        @pl.when(is_panel)
        def _():
            assemble(t, store)

        @pl.when(jnp.logical_not(is_panel))
        def _():
            assemble_here(t)

    def second(t):
        if t < SUB - 1:
            sent_part(t + 1)
        send_part(SUB + t)

    def p_copy(i, k, t):
        at = pl.ds(pl.multiple_of(PANEL + t * SPAN + (x_hi + 2 * k) * PART, PART), PART)
        return pltpu.make_async_remote_copy(
            src_ref=panel.at[:, at],
            dst_ref=psbuf.at[k, :, pl.ds(t * PART, PART)],
            send_sem=p_send.at[(t * 2 + k) * NR + i],
            recv_sem=p_recv.at[t * 2 + k],
            device_id={"row": (r + i) % NR},
            device_id_type=MESH,
        )

    def send_rows(t):
        from_sibling(LEAD + t * TURN)

        @pl.when(is_root)
        def _():
            @pl.loop(1, NR)
            def _(i):
                for k in range(2):
                    p_copy(i, k, t).start()

            for k in range(2):
                at = pl.ds(pl.multiple_of(PANEL + t * SPAN + (x_hi + 2 * k) * PART, PART), PART)
                psbuf[k, :, t * PART : (t + 1) * PART, :] = panel[:, at, :]

    forward_all(0, LEAD)
    phase(0)
    forward_all(LEAD, LEAD + TURN // 2)
    second(0)
    forward_all(LEAD + TURN // 2, LEAD + TURN)
    phase(1)
    forward_all(LEAD + TURN, LEAD + TURN + TURN // 2)
    second(1)
    forward_all(LEAD + TURN + TURN // 2, AHEAD)
    for i in range(LEAD):
        from_sibling(i)

    send_rows(0)
    for i in range(4):
        for j in range(4):
            rows = slice(i * BLK, (i + 1) * BLK)
            cols = slice(j * BLK, (j + 1) * BLK)
            smat[rows, cols] = 0.5 * (panel[j, rows, :] + panel[i, cols, :].T)

    @pl.loop(0, 4)
    def _(b):
        for t in range(2, SUB):

            @pl.when(b == t - 2)
            def _():
                phase(t)

        at = pl.ds(pl.multiple_of(b * BLK, BLK), BLK)
        block[...] = smat[at, at]
        for k in range(1, 4):

            @pl.when(b == k)
            def _():
                x = xmat[: k * BLK, : k * BLK]
                lb = nt(smat[k * BLK : (k + 1) * BLK, : k * BLK], x, HI)
                block[...] -= nt(lb, lb, HI)
                lbx[:, : k * BLK] = nn(lb, x, HI)

        def between(n):
            first = AHEAD + 8 * b + 2 * n
            forward_all(first, first + 2)
            @pl.when((b == 0) & (n == 2))
            def _():
                second(2)

            @pl.when((b == 1) & (n == 1))
            def _():
                second(3)

            for t in range(1, SUB):
                due = LEAD + t * TURN + 4 * LAG - AHEAD - 1
                due = -(-due // 2)

                @pl.when(4 * b + n == due)
                def _():
                    send_rows(t)

        v = inverse_of_factor(block[...], between)
        for k in range(1, 4):

            @pl.when(b == k)
            def _():
                xmat[k * BLK : (k + 1) * BLK, : k * BLK] = -nn(v, lbx[:, : k * BLK], HI)

        xmat[at, at] = v

    last = AHEAD + 32
    forward_all(last, last + 2)

    @pl.when(jnp.logical_not(is_root))
    def _():
        for t in range(SUB):
            for k in range(2):
                p_copy(0, k, t).wait_recv()

    x_high, x_low = split(xmat[...])

    def three(product, a, high, low):
        a_high, a_low = split(a)
        return product(a_high, high) + (product(a_high, low) + product(a_low, high))

    for k in range(2):
        ps = jnp.concatenate([psbuf[k, s] for s in range(4)], axis=1)
        wt = three(nn, three(nt, ps, x_high, x_low), x_high, x_low)
        if k == 0:
            at = pl.ds(pl.multiple_of((c % 4) * BLK, BLK), BLK)
            wt = jnp.where(is_panel, -xmat[at, :], wt)
        high, low = split(wt)
        wth[k * BLK : (k + 1) * BLK, :] = high
        wtl[k * BLK : (k + 1) * BLK, :] = low

    forward_all(last + 2, last + 3)

    for t in range(SUB, 2 * SUB):
        got_part(t)
        assemble_here(t)

    forward_all(last + 3, last + 4)
    drop = is_panel & (lax.broadcasted_iota(jnp.int32, (1, 2 * BLK), 1) < BLK)

    def out_copy(t, u):
        return pltpu.make_async_copy(
            acc.at[pl.ds(u * UNIT, UNIT), pl.ds(t * PART, PART)],
            out.at[pl.ds(u * UNIT, UNIT), pl.ds(t * PART, PART)],
            out_sem.at[t * 4 + u],
        )

    def update(t):
        @pl.loop(1, TURN)
        def _(i):
            from_sibling(LEAD + t * TURN + i)

        @pl.loop(0, KR // UNIT)
        def _(u):
            first = pl.multiple_of(PANEL + t * SPAN + u * UNIT * PART, PART)
            rows = jnp.concatenate(
                [panel[s, pl.ds(first, UNIT * PART), :] for s in range(4)], axis=1
            )
            lead_at = pl.ds(pl.multiple_of((r % 4) * BLK + t * PART, PART), PART)
            head = jnp.where(is_lead & (u == 0), smat[lead_at, :], rows[:PART])
            rows = jnp.concatenate([head, rows[PART:]], axis=0)
            high, low = split(rows)
            total = nt(high, wth[...]) + (nt(high, wtl[...]) + nt(low, wth[...]))
            for b in range(UNIT):
                at = u * UNIT + b
                part = slice(t * PART, (t + 1) * PART)
                acc[at, part, :] = (
                    jnp.where(drop, 0.0, acc[at, part, :]) - total[b * PART : (b + 1) * PART]
                )
            out_copy(t, u).start()

    update(0)
    forward_all(last + 4, last + 5)
    update(1)
    forward_all(last + 5, STEPS)
    update(2)
    update(3)

    for t in range(SUB):

        @pl.loop(0, KR // UNIT)
        def _(u):
            out_copy(t, u).wait()

        sent_part(SUB + t)

    @pl.when(is_panel)
    def _():
        @pl.loop(0, LEAD)
        def _(d):
            @pl.when(d != r)
            def _():
                se_copy(d).wait_send()

    @pl.when(is_panel & is_lead)
    def _():
        @pl.loop(1, NR)
        def _(i):
            s_copy(i).wait_send()

    @pl.when(is_root)
    def _():
        @pl.loop(1, NR)
        def _(i):
            for t in range(SUB):
                for k in range(2):
                    p_copy(i, k, t).wait_send()

    for g in range(2):

        @pl.loop(0, NCH)
        def _(i):
            @pl.when((c != 2 * g + core) | (i >= NCH - WINDOW))
            def _():
                sent(g, i)


def tables(row_map, col_map):
    my_row = lax.axis_index("row")
    my_col = lax.axis_index("col")
    layout = row_map.reshape(NR, -1)
    count = layout.shape[1]
    owner = layout % NR
    counter = jnp.arange(count)
    earlier = (owner[:, :, None] == owner[:, None, :]) & (
        counter[None, None, :] < counter[None, :, None]
    )
    rank = jnp.sum(earlier.astype(jnp.int32), axis=2)
    slot_out = owner * MOST + rank
    mine = lax.dynamic_index_in_dim(slot_out, my_row, 0, keepdims=False)
    send = jnp.sum(
        jnp.where(mine[None, :] == jnp.arange(SLOTS)[:, None], counter[None, :], 0), axis=1
    )
    slot_in = (jnp.arange(NR)[:, None] * MOST + rank).reshape(2, -1)
    wanted = jnp.arange(KR) * NR + my_row
    hit = layout.reshape(2, 1, -1) == wanted[None, :, None]
    receive = SLOTS + jnp.sum(jnp.where(hit, slot_in[:, None, :] - SLOTS, 0), axis=2)
    child = my_row // (NR // 2)
    first = lax.dynamic_index_in_dim(
        col_map.reshape(2, NC, 2)[:, :, 0].reshape(-1), child * NC + my_col, 0
    )
    own = lax.dynamic_index_in_dim(layout, my_row, 0, keepdims=False)
    lead = jnp.sum(
        jnp.where(own[None, :] == jnp.arange(LEAD)[:, None], counter[None, :] + 1, 0), axis=1
    )
    return jnp.concatenate([send, receive.reshape(-1), first // NC, lead]).astype(jnp.int32)


def local(front, children, row_map, col_map):
    table = tables(row_map, col_map)
    hbm = pl.BlockSpec(memory_space=pl.ANY)
    blocks = children.reshape(-1, BLK, 2 * BLK)
    tile = (BLK, BLK)
    held = front.reshape(KR, BLK, 2 * BLK)
    vmem = lambda *shape: pltpu.VMEM(shape, F32)
    dma = lambda count: pltpu.SemaphoreType.DMA((count,))
    result = pl.pallas_call(
        kernel,
        out_shape=jax.ShapeDtypeStruct(held.shape, F32),
        in_specs=[pl.BlockSpec(memory_space=pltpu.SMEM), hbm, hbm],
        out_specs=hbm,
        scratch_shapes=[
            vmem(*blocks.shape),
            vmem(*held.shape),
            vmem(SLOTS, *tile),
            vmem(SLOTS, *tile),
            *[vmem(SLOTS + 1, PART, BLK) for _ in range(2 * SUB)],
            vmem(LEAD, *tile),
            vmem(NR, *tile),
            vmem(4, NCH * BLK, BLK),
            vmem(2, 4, *tile),
            vmem(PANEL, PANEL),
            vmem(PANEL, PANEL),
            vmem(*tile),
            vmem(BLK, PANEL),
            pltpu.VMEM((2 * BLK, PANEL), BF16),
            pltpu.VMEM((2 * BLK, PANEL), BF16),
            dma(2),
            dma(2 * SUB * NR),
            dma(2 * SUB * NR),
            dma(2 * SUB),
            dma(16 * NCH),
            dma(4 * NCH),
            dma(LEAD),
            dma(NR),
            dma(NR),
            dma(LEAD),
            dma(2 * SUB * NR),
            dma(2 * SUB),
            dma(16),
        ],
        compiler_params=pltpu.CompilerParams(
            collective_id=0, has_side_effects=True, vmem_limit_bytes=60 * 2**20
        ),
    )(table, held, blocks)
    return result.reshape(front.shape)


def solution(mesh):
    placed = (P("row", "col"), P("row", "col"), P(), P())
    return jax.shard_map(
        local, mesh=mesh, in_specs=placed, out_specs=P("row", "col"), check_vma=False
    )
```

```python
import jax
import jax.numpy as jnp
from jax import lax
from jax.experimental import pallas as pl
from jax.experimental.pallas import tpu as pltpu
from jax.sharding import PartitionSpec as P

BLK = 128
PANEL = 512
NR = 8
NC = 16
MOST = 8
SLOTS = NR * MOST
KR = 44
SUB = 4
PART = BLK // SUB
SPAN = KR * PART
NCH = (PANEL + KR * BLK) // BLK
LEAD = PANEL // BLK
TURN = SPAN // BLK
UNIT = 11
WINDOW = 6
LAG = 4
SEND_5 = 3
SEND_6 = 12
SEND_7 = 14
STEPS = NCH + 4 * LAG
AHEAD = LEAD + 2 * TURN
HI = lax.Precision.HIGHEST
MESH = pl.DeviceIdType.MESH
F32 = jnp.float32
BF16 = jnp.bfloat16


def nt(a, b, precision=None):
    return lax.dot_general(
        a, b, (((1,), (1,)), ((), ())), precision=precision, preferred_element_type=F32
    )


def nn(a, b, precision=None):
    return lax.dot_general(
        a, b, (((1,), (0,)), ((), ())), precision=precision, preferred_element_type=F32
    )


def split(x):
    high = x.astype(BF16)
    return high, (x - high.astype(F32)).astype(BF16)


def inverse_of_factor(a, between):
    rows = lax.broadcasted_iota(jnp.int32, (BLK, 1), 0)
    eye = rows == lax.broadcasted_iota(jnp.int32, (BLK, BLK), 1)
    e = eye.astype(F32)
    done_a, done_e = [], []
    for first in range(0, BLK, 32):
        below = rows[first:]
        for j in range(first, first + 32):
            i = j - first
            pivot = 1.0 / a[i : i + 1, j : j + 1]
            col = jnp.where(below > j, a[:, j : j + 1], 0.0)
            row_a = a[i : i + 1, :] * pivot
            row_e = e[i : i + 1, :] * pivot
            a = a - col * row_a
            e = e - col * row_e
        done_a.append(a[:32])
        done_e.append(e[:32])
        a, e = a[32:], e[32:]
        between(first // 32)
    a = jnp.concatenate(done_a, axis=0)
    e = jnp.concatenate(done_e, axis=0)
    d = jnp.sum(jnp.where(eye, a, 0.0), axis=1, keepdims=True)
    s = lax.rsqrt(d)
    s = s * (1.5 - 0.5 * d * s * s)
    return e * s


def kernel(
    tbl, front, children_hbm, out,
    children, acc, stage0, stage1, in00, in01, in02, in03, in10, in11, in12, in13, stage_s, in_s, panel, psbuf, smat, xmat, block, lbx, wth, wtl,
    load_sem, ex_send, ex_recv, own_sem, bc_send, bc_recv, se_send, se_recv, s_send, s_recv, p_send, p_recv, out_sem,
):
    r = lax.axis_index("row")
    c = lax.axis_index("col")
    x_hi = c // 8
    y = (c // 2) % 4
    core = c % 2
    is_panel = c < 4
    is_lead = r < 4
    is_root = r == c % NR
    ins = (in00, in01, in02, in03, in10, in11, in12, in13)

    load_children = pltpu.make_async_copy(children_hbm, children, load_sem.at[0])
    load_front = pltpu.make_async_copy(front, acc, load_sem.at[1])
    load_children.start()
    load_front.start()

    barrier = pltpu.get_barrier_semaphore()

    @pl.loop(1, NR)
    def _(i):
        pl.semaphore_signal(barrier, inc=1, device_id={"row": (r + i) % NR}, device_id_type=MESH)

    @pl.loop(1, NC)
    def _(i):
        pl.semaphore_signal(barrier, inc=1, device_id={"col": (c + i) % NC}, device_id_type=MESH)

    swap = tbl[SLOTS + 2 * KR] == 1

    def ex_parts(t, slots):
        at = pl.ds(t % SUB * PART, PART)
        return (stage0 if t < SUB else stage1).at[slots, at]

    def ex_copy(t, i):
        to = (r + i) % NR
        return pltpu.make_async_remote_copy(
            src_ref=ex_parts(t, pl.ds(to * MOST, MOST)),
            dst_ref=ins[t].at[pl.ds(r * MOST, MOST)],
            send_sem=ex_send.at[t * NR + i],
            recv_sem=ex_recv.at[t * NR + i],
            device_id={"row": to},
            device_id_type=MESH,
        )

    def own_copy(t):
        mine = pl.ds(r * MOST, MOST)
        return pltpu.make_async_copy(ex_parts(t, mine), ins[t].at[mine], own_sem.at[t])

    def send_part(t):
        own_copy(t).start()

        @pl.loop(1, NR)
        def _(i):
            ex_copy(t, i).start()

    def sent_part(t):
        @pl.loop(1, NR)
        def _(i):
            ex_copy(t, i).wait_send()

    def got_part(t):
        own_copy(t).wait()

        @pl.loop(1, NR)
        def _(i):
            ex_copy(t, i).wait_recv()

    def se_copy(d):
        return pltpu.make_async_remote_copy(
            src_ref=stage_s.at[d],
            dst_ref=in_s.at[r],
            send_sem=se_send.at[d],
            recv_sem=se_recv.at[r],
            device_id={"row": d},
            device_id_type=MESH,
        )

    def se_wait(source):
        pltpu.make_async_remote_copy(
            src_ref=stage_s.at[0],
            dst_ref=in_s.at[source],
            send_sem=se_send.at[0],
            recv_sem=se_recv.at[source],
            device_id={"row": r},
            device_id_type=MESH,
        ).wait_recv()

    load_children.wait()

    @pl.loop(0, LEAD)
    def _(d):
        found = tbl[SLOTS + 2 * KR + 1 + d]
        block = children[jnp.maximum(found - 1, 0)]
        half = jnp.where(swap, block[:, BLK:], block[:, :BLK])
        stage_s[d] = jnp.where(found > 0, half, 0.0)

    pl.semaphore_wait(barrier, NR - 1 + NC - 1)

    @pl.when(is_panel)
    def _():
        @pl.loop(0, LEAD)
        def _(d):
            @pl.when(d != r)
            def _():
                se_copy(d).start()

    @pl.loop(0, SLOTS)
    def _(slot):
        block = children[tbl[slot]]
        stage0[slot] = jnp.where(swap, block[:, BLK:], block[:, :BLK])

    send_part(0)
    for t in range(2 * SUB):
        ins[t][SLOTS] = jnp.zeros((PART, BLK), F32)

    @pl.loop(0, SLOTS)
    def _(slot):
        block = children[tbl[slot]]
        stage1[slot] = jnp.where(swap, block[:, :BLK], block[:, BLK:])

    @pl.when(jnp.logical_not(is_panel))
    def _():
        send_part(1)

    xmat[...] = jnp.zeros_like(xmat)
    load_front.wait()

    def s_copy(i):
        at = pl.ds(pl.multiple_of(r * BLK, BLK), BLK)
        return pltpu.make_async_remote_copy(
            src_ref=panel.at[c, at],
            dst_ref=panel.at[c, at],
            send_sem=s_send.at[i],
            recv_sem=s_recv.at[r],
            device_id={"row": (r + i) % NR},
            device_id_type=MESH,
        )

    def s_wait(source):
        at = pl.ds(pl.multiple_of(source * BLK, BLK), BLK)
        pltpu.make_async_remote_copy(
            src_ref=panel.at[c, at],
            dst_ref=panel.at[c, at],
            send_sem=s_send.at[0],
            recv_sem=s_recv.at[source],
            device_id={"row": r},
            device_id_type=MESH,
        ).wait_recv()

    @pl.when(is_panel & is_lead)
    def _():
        in_s[r] = stage_s[r]

        @pl.loop(0, NR)
        def _(source):
            @pl.when(source != r)
            def _():
                se_wait(source)

        total = acc[0, :, :BLK]
        for source in range(NR):
            total = total + in_s[source]
        panel[c, pl.ds(pl.multiple_of(r * BLK, BLK), BLK), :] = total

        @pl.loop(1, NR)
        def _(i):
            s_copy(i).start()

    @pl.when(is_panel)
    def _():
        send_part(1)

        @pl.loop(0, LEAD)
        def _(source):
            @pl.when(source != r)
            def _():
                s_wait(source)

    def bc_copy(s, i, d, to):
        at = pl.ds(pl.multiple_of(i * BLK, BLK), BLK)
        return pltpu.make_async_remote_copy(
            src_ref=panel.at[s, at],
            dst_ref=panel.at[s, at],
            send_sem=bc_send.at[(s * 4 + d) * NCH + i],
            recv_sem=bc_recv.at[s * NCH + i],
            device_id={"col": to},
            device_id_type=MESH,
        )

    def targets(g, i):
        yp = y if g == 0 else (5 - y) % 4
        even = i % 2 == 0
        odd = i % 2 == 1
        up, down = (yp + 1) % 4, (yp + 3) % 4
        y_up = up if g == 0 else (5 - up) % 4
        y_down = down if g == 0 else (5 - down) % 4
        here, there = x_hi == 0, x_hi == 1
        return (
            (
                (here & (yp == 0)) | (there & ((even & (yp == 0)) | (odd & (yp == 3)))),
                x_hi * 8 + y_up * 2 + core,
            ),
            (
                (yp == 3) | ((yp == 0) & (here | even)) | (there & odd & (yp == 2)),
                x_hi * 8 + y_down * 2 + core,
            ),
            (
                here & ((even & (yp == 0)) | (odd & (yp == 3))),
                8 + y * 2 + core,
            ),
            (core >= 0, x_hi * 8 + y * 2 + 1 - core),
        )

    def sent(g, i):
        for d, (when, to) in enumerate(targets(g, i)):

            @pl.when(when)
            def _():
                bc_copy(2 * g + core, i, d, to).wait_send()

    def forward(step):
        odd = step % 2
        for g in range(2):
            s = 2 * g + core
            yp = y if g == 0 else (5 - y) % 4
            near = jnp.where(yp == 0, 0, jnp.where(yp == 2, 2, 1))
            far_odd = jnp.where(yp == 3, 2, jnp.where(yp == 1, 4, 3))
            far = jnp.where(odd == 1, far_odd, near + 1)
            i = step - LAG * jnp.where(x_hi == 0, near, far)

            @pl.when((i >= 0) & (i < NCH))
            def _():
                @pl.when(c != s)
                def _():
                    bc_copy(s, i, 0, c).wait_recv()

                @pl.when((c == s) & (i >= WINDOW))
                def _():
                    sent(g, i - WINDOW)

                for d, (when, to) in enumerate(targets(g, i)):

                    @pl.when(when)
                    def _():
                        bc_copy(s, i, d, to).start()

    def from_sibling(i):
        for g in range(2):
            s = 2 * g + 1 - core
            bc_copy(s, i, 0, c).wait_recv()

    def forward_all(first, last):
        @pl.loop(first, last)
        def _(step):
            forward(step)

    def assemble(t, store):
        q, part = t // SUB, pl.ds(t % SUB * PART, PART)

        @pl.loop(0, KR)
        def _(k):
            total = (
                acc[k, part, q * BLK : (q + 1) * BLK]
                + ins[t][tbl[SLOTS + k]]
                + ins[t][tbl[SLOTS + KR + k]]
            )
            store(k, total)

    def assemble_here(t):
        q, part = t // SUB, pl.ds(t % SUB * PART, PART)

        def store(k, total):
            acc[k, part, q * BLK : (q + 1) * BLK] = total

        assemble(t, store)

    def phase(t):
        if t < 2:
            send_part(t + 2)
        got_part(t)

        def store(k, total):
            at = pl.ds(pl.multiple_of(PANEL + t * SPAN + k * PART, PART), PART)
            panel[c, at, :] = total

        @pl.when(is_panel)
        def _():
            assemble(t, store)

        @pl.when(jnp.logical_not(is_panel))
        def _():
            assemble_here(t)

    other = r + 1 - 2 * (r % 2)
    is_relay = other == c % NR

    def p_rows(k, t):
        return pl.ds(pl.multiple_of(PANEL + t * SPAN + (x_hi + 2 * k) * PART, PART), PART)

    def p_copy(i, k, t, relayed=False):
        to = jnp.where(i < 4, r, other)
        to = jnp.where(i == 0, other, (to + 2 * (i % 4)) % NR)
        part = pl.ds(t * PART, PART)
        return pltpu.make_async_remote_copy(
            src_ref=psbuf.at[k, :, part] if relayed else panel.at[:, p_rows(k, t)],
            dst_ref=psbuf.at[k, :, part],
            send_sem=p_send.at[(t * 2 + k) * NR + i],
            recv_sem=p_recv.at[t * 2 + k],
            device_id={"row": to},
            device_id_type=MESH,
        )

    def p_each(t, act):
        @pl.when(is_root)
        def _():
            @pl.loop(0, 4)
            def _(i):
                for k in range(2):
                    act(p_copy(i, k, t))

            if t == SUB - 1:

                @pl.loop(5, 8)
                def _(i):
                    for k in range(2):
                        act(p_copy(i, k, t))

    def p_relay(t, act):
        @pl.loop(1, 4)
        def _(i):
            for k in range(2):
                act(p_copy(i, k, t, True))

    def send_rows(t):
        from_sibling(LEAD + t * TURN)
        p_each(t, lambda copy: copy.start())

        @pl.when(is_root)
        def _():
            for k in range(2):
                psbuf[k, :, t * PART : (t + 1) * PART, :] = panel[:, p_rows(k, t), :]

        if t > 0:

            @pl.when(is_relay)
            def _():
                for k in range(2):
                    p_copy(0, k, t - 1).wait_recv()
                p_relay(t - 1, lambda copy: copy.start())

    forward_all(0, LEAD)
    phase(0)
    forward_all(LEAD, LEAD + TURN)
    phase(1)
    forward_all(LEAD + TURN, LEAD + TURN + TURN // 2)
    send_part(SUB)
    forward_all(LEAD + TURN + TURN // 2, AHEAD)
    for i in range(LEAD):
        from_sibling(i)

    send_rows(0)
    for i in range(4):
        for j in range(4):
            rows = slice(i * BLK, (i + 1) * BLK)
            cols = slice(j * BLK, (j + 1) * BLK)
            smat[rows, cols] = 0.5 * (panel[j, rows, :] + panel[i, cols, :].T)

    @pl.loop(0, 4)
    def _(b):
        for t in range(2, SUB):

            @pl.when(b == t - 2)
            def _():
                phase(t)

        at = pl.ds(pl.multiple_of(b * BLK, BLK), BLK)
        block[...] = smat[at, at]
        for k in range(1, 4):

            @pl.when(b == k)
            def _():
                x = xmat[: k * BLK, : k * BLK]
                lb = nt(smat[k * BLK : (k + 1) * BLK, : k * BLK], x, HI)
                block[...] -= nt(lb, lb, HI)
                lbx[:, : k * BLK] = nn(lb, x, HI)

        def between(n):
            first = AHEAD + 8 * b + 2 * n
            forward_all(first, first + 2)
            for t, point in enumerate((SEND_5, SEND_6, SEND_7)):

                @pl.when(4 * b + n == point)
                def _():
                    send_part(SUB + 1 + t)

            for t in range(1, SUB):
                due = LEAD + t * TURN + 4 * LAG - AHEAD - 1
                due = -(-due // 2)

                @pl.when(4 * b + n == due)
                def _():
                    send_rows(t)

        v = inverse_of_factor(block[...], between)
        for k in range(1, 4):

            @pl.when(b == k)
            def _():
                xmat[k * BLK : (k + 1) * BLK, : k * BLK] = -nn(v, lbx[:, : k * BLK], HI)

        xmat[at, at] = v

    last = AHEAD + 32
    forward_all(last, last + 2)

    for t in range(SUB):

        @pl.when(jnp.logical_not(is_root | (is_relay & (t < SUB - 1))))
        def _():
            for k in range(2):
                p_copy(0, k, t).wait_recv()

    x_high, x_low = split(xmat[...])

    def three(product, a, high, low):
        a_high, a_low = split(a)
        return product(a_high, high) + (product(a_high, low) + product(a_low, high))

    for k in range(2):
        ps = jnp.concatenate([psbuf[k, s] for s in range(4)], axis=1)
        wt = three(nn, three(nt, ps, x_high, x_low), x_high, x_low)
        if k == 0:
            at = pl.ds(pl.multiple_of((c % 4) * BLK, BLK), BLK)
            wt = jnp.where(is_panel, -xmat[at, :], wt)
        high, low = split(wt)
        wth[k * BLK : (k + 1) * BLK, :] = high
        wtl[k * BLK : (k + 1) * BLK, :] = low

    forward_all(last + 2, last + 3)

    drop = is_panel & (lax.broadcasted_iota(jnp.int32, (1, 2 * BLK), 1) < BLK)

    def out_copy(t, u):
        return pltpu.make_async_copy(
            acc.at[pl.ds(u * UNIT, UNIT), pl.ds(t * PART, PART)],
            out.at[pl.ds(u * UNIT, UNIT), pl.ds(t * PART, PART)],
            out_sem.at[t * 4 + u],
        )

    def update(t):
        @pl.loop(1, TURN)
        def _(i):
            from_sibling(LEAD + t * TURN + i)

        @pl.loop(0, KR // UNIT)
        def _(u):
            first = pl.multiple_of(PANEL + t * SPAN + u * UNIT * PART, PART)
            rows = jnp.concatenate(
                [panel[s, pl.ds(first, UNIT * PART), :] for s in range(4)], axis=1
            )
            lead_at = pl.ds(pl.multiple_of((r % 4) * BLK + t * PART, PART), PART)
            head = jnp.where(is_lead & (u == 0), smat[lead_at, :], rows[:PART])
            rows = jnp.concatenate([head, rows[PART:]], axis=0)
            high, low = split(rows)
            total = nt(high, wth[...]) + (nt(high, wtl[...]) + nt(low, wth[...]))
            for b in range(UNIT):
                at = u * UNIT + b
                part = slice(t * PART, (t + 1) * PART)
                acc[at, part, :] = (
                    jnp.where(drop, 0.0, acc[at, part, :]) - total[b * PART : (b + 1) * PART]
                )

    update(0)
    forward_all(last + 3, last + 5)
    update(1)
    forward_all(last + 5, STEPS)
    update(2)
    update(3)

    for t in range(SUB):
        got_part(SUB + t)
        assemble_here(SUB + t)

        @pl.loop(0, KR // UNIT)
        def _(u):
            out_copy(t, u).start()

    for t in range(SUB):

        @pl.loop(0, KR // UNIT)
        def _(u):
            out_copy(t, u).wait()

        sent_part(t)
        sent_part(SUB + t)

    @pl.when(is_panel)
    def _():
        @pl.loop(0, LEAD)
        def _(d):
            @pl.when(d != r)
            def _():
                se_copy(d).wait_send()

    @pl.when(is_panel & is_lead)
    def _():
        @pl.loop(1, NR)
        def _(i):
            s_copy(i).wait_send()

    for t in range(SUB):
        p_each(t, lambda copy: copy.wait_send())
        if t < SUB - 1:

            @pl.when(is_relay)
            def _():
                p_relay(t, lambda copy: copy.wait_send())

    for g in range(2):

        @pl.loop(0, NCH)
        def _(i):
            @pl.when((c != 2 * g + core) | (i >= NCH - WINDOW))
            def _():
                sent(g, i)


def tables(row_map, col_map):
    my_row = lax.axis_index("row")
    my_col = lax.axis_index("col")
    layout = row_map.reshape(NR, -1)
    count = layout.shape[1]
    owner = layout % NR
    counter = jnp.arange(count)
    earlier = (owner[:, :, None] == owner[:, None, :]) & (
        counter[None, None, :] < counter[None, :, None]
    )
    rank = jnp.sum(earlier.astype(jnp.int32), axis=2)
    slot_out = owner * MOST + rank
    mine = lax.dynamic_index_in_dim(slot_out, my_row, 0, keepdims=False)
    send = jnp.sum(
        jnp.where(mine[None, :] == jnp.arange(SLOTS)[:, None], counter[None, :], 0), axis=1
    )
    slot_in = (jnp.arange(NR)[:, None] * MOST + rank).reshape(2, -1)
    wanted = jnp.arange(KR) * NR + my_row
    hit = layout.reshape(2, 1, -1) == wanted[None, :, None]
    receive = SLOTS + jnp.sum(jnp.where(hit, slot_in[:, None, :] - SLOTS, 0), axis=2)
    child = my_row // (NR // 2)
    first = lax.dynamic_index_in_dim(
        col_map.reshape(2, NC, 2)[:, :, 0].reshape(-1), child * NC + my_col, 0
    )
    own = lax.dynamic_index_in_dim(layout, my_row, 0, keepdims=False)
    lead = jnp.sum(
        jnp.where(own[None, :] == jnp.arange(LEAD)[:, None], counter[None, :] + 1, 0), axis=1
    )
    return jnp.concatenate([send, receive.reshape(-1), first // NC, lead]).astype(jnp.int32)


def local(front, children, row_map, col_map):
    table = tables(row_map, col_map)
    hbm = pl.BlockSpec(memory_space=pl.ANY)
    blocks = children.reshape(-1, BLK, 2 * BLK)
    tile = (BLK, BLK)
    held = front.reshape(KR, BLK, 2 * BLK)
    vmem = lambda *shape: pltpu.VMEM(shape, F32)
    dma = lambda count: pltpu.SemaphoreType.DMA((count,))
    result = pl.pallas_call(
        kernel,
        out_shape=jax.ShapeDtypeStruct(held.shape, F32),
        in_specs=[pl.BlockSpec(memory_space=pltpu.SMEM), hbm, hbm],
        out_specs=hbm,
        scratch_shapes=[
            vmem(*blocks.shape),
            vmem(*held.shape),
            vmem(SLOTS, *tile),
            vmem(SLOTS, *tile),
            *[vmem(SLOTS + 1, PART, BLK) for _ in range(2 * SUB)],
            vmem(LEAD, *tile),
            vmem(NR, *tile),
            vmem(4, NCH * BLK, BLK),
            vmem(2, 4, *tile),
            vmem(PANEL, PANEL),
            vmem(PANEL, PANEL),
            vmem(*tile),
            vmem(BLK, PANEL),
            pltpu.VMEM((2 * BLK, PANEL), BF16),
            pltpu.VMEM((2 * BLK, PANEL), BF16),
            dma(2),
            dma(2 * SUB * NR),
            dma(2 * SUB * NR),
            dma(2 * SUB),
            dma(16 * NCH),
            dma(4 * NCH),
            dma(LEAD),
            dma(NR),
            dma(NR),
            dma(LEAD),
            dma(2 * SUB * NR),
            dma(2 * SUB),
            dma(16),
        ],
        compiler_params=pltpu.CompilerParams(
            collective_id=0, has_side_effects=True, vmem_limit_bytes=60 * 2**20
        ),
    )(table, held, blocks)
    return result.reshape(front.shape)


def solution(mesh):
    placed = (P("row", "col"), P("row", "col"), P(), P())
    return jax.shard_map(
        local, mesh=mesh, in_specs=placed, out_specs=P("row", "col"), check_vma=False
    )
```

```python
import jax
import jax.numpy as jnp
from jax import lax
from jax.experimental import pallas as pl
from jax.experimental.pallas import tpu as pltpu
from jax.sharding import PartitionSpec as P

BLK = 128
PANEL = 512
NR = 8
NC = 16
MOST = 8
SLOTS = NR * MOST
KR = 44
SUB = 4
PART = BLK // SUB
SPAN = KR * PART
NCH = (PANEL + KR * BLK) // BLK
LEAD = PANEL // BLK
TURN = SPAN // BLK
UNIT = 11
WINDOW = 6
LAG = 4
SEND_5 = 1
SEND_6 = 5
SEND_7 = 9
STEPS = NCH + 4 * LAG
AHEAD = LEAD + 2 * TURN
HI = lax.Precision.HIGHEST
MESH = pl.DeviceIdType.MESH
F32 = jnp.float32
BF16 = jnp.bfloat16


def nt(a, b, precision=None):
    return lax.dot_general(
        a, b, (((1,), (1,)), ((), ())), precision=precision, preferred_element_type=F32
    )


def nn(a, b, precision=None):
    return lax.dot_general(
        a, b, (((1,), (0,)), ((), ())), precision=precision, preferred_element_type=F32
    )


def split(x):
    high = x.astype(BF16)
    return high, (x - high.astype(F32)).astype(BF16)


def inverse_of_factor(a, between):
    rows = lax.broadcasted_iota(jnp.int32, (BLK, 1), 0)
    eye = rows == lax.broadcasted_iota(jnp.int32, (BLK, BLK), 1)
    e = eye.astype(F32)
    done_a, done_e = [], []
    for first in range(0, BLK, 32):
        below = rows[first:]
        for j in range(first, first + 32):
            i = j - first
            pivot = 1.0 / a[i : i + 1, j : j + 1]
            col = jnp.where(below > j, a[:, j : j + 1], 0.0)
            row_a = a[i : i + 1, :] * pivot
            row_e = e[i : i + 1, :] * pivot
            a = a - col * row_a
            e = e - col * row_e
        done_a.append(a[:32])
        done_e.append(e[:32])
        a, e = a[32:], e[32:]
        between(first // 32)
    a = jnp.concatenate(done_a, axis=0)
    e = jnp.concatenate(done_e, axis=0)
    d = jnp.sum(jnp.where(eye, a, 0.0), axis=1, keepdims=True)
    s = lax.rsqrt(d)
    s = s * (1.5 - 0.5 * d * s * s)
    return e * s


def kernel(
    tbl, front, children_hbm, out,
    children, acc, stage0, stage1, in00, in01, in02, in03, in10, in11, in12, in13, stage_s, in_s, panel, psbuf, smat, xmat, block, lbx, wth, wtl,
    load_sem, ex_send, ex_recv, own_sem, bc_send, bc_recv, se_send, se_recv, s_send, s_recv, p_send, p_recv, out_sem,
):
    r = lax.axis_index("row")
    c = lax.axis_index("col")
    x_hi = c // 8
    y = (c // 2) % 4
    core = c % 2
    is_panel = c < 4
    is_lead = r < 4
    is_root = r == c % NR
    ins = (in00, in01, in02, in03, in10, in11, in12, in13)

    load_children = pltpu.make_async_copy(children_hbm, children, load_sem.at[0])
    load_front = pltpu.make_async_copy(front, acc, load_sem.at[1])
    load_children.start()
    load_front.start()

    barrier = pltpu.get_barrier_semaphore()

    @pl.loop(1, NR)
    def _(i):
        pl.semaphore_signal(barrier, inc=1, device_id={"row": (r + i) % NR}, device_id_type=MESH)

    @pl.loop(1, NC)
    def _(i):
        pl.semaphore_signal(barrier, inc=1, device_id={"col": (c + i) % NC}, device_id_type=MESH)

    swap = tbl[SLOTS + 2 * KR] == 1

    def ex_parts(t, slots):
        at = pl.ds(t % SUB * PART, PART)
        return (stage0 if t < SUB else stage1).at[slots, at]

    def ex_copy(t, i):
        to = (r + i) % NR
        return pltpu.make_async_remote_copy(
            src_ref=ex_parts(t, pl.ds(to * MOST, MOST)),
            dst_ref=ins[t].at[pl.ds(r * MOST, MOST)],
            send_sem=ex_send.at[t * NR + i],
            recv_sem=ex_recv.at[t * NR + i],
            device_id={"row": to},
            device_id_type=MESH,
        )

    def own_copy(t):
        mine = pl.ds(r * MOST, MOST)
        return pltpu.make_async_copy(ex_parts(t, mine), ins[t].at[mine], own_sem.at[t])

    def send_part(t):
        own_copy(t).start()

        @pl.loop(1, NR)
        def _(i):
            ex_copy(t, i).start()

    def sent_part(t):
        @pl.loop(1, NR)
        def _(i):
            ex_copy(t, i).wait_send()

    def got_part(t):
        own_copy(t).wait()

        @pl.loop(1, NR)
        def _(i):
            ex_copy(t, i).wait_recv()

    def se_copy(d):
        return pltpu.make_async_remote_copy(
            src_ref=stage_s.at[d],
            dst_ref=in_s.at[r],
            send_sem=se_send.at[d],
            recv_sem=se_recv.at[r],
            device_id={"row": d},
            device_id_type=MESH,
        )

    def se_wait(source):
        pltpu.make_async_remote_copy(
            src_ref=stage_s.at[0],
            dst_ref=in_s.at[source],
            send_sem=se_send.at[0],
            recv_sem=se_recv.at[source],
            device_id={"row": r},
            device_id_type=MESH,
        ).wait_recv()

    load_children.wait()

    @pl.loop(0, LEAD)
    def _(d):
        found = tbl[SLOTS + 2 * KR + 1 + d]
        block = children[jnp.maximum(found - 1, 0)]
        half = jnp.where(swap, block[:, BLK:], block[:, :BLK])
        stage_s[d] = jnp.where(found > 0, half, 0.0)

    pl.semaphore_wait(barrier, NR - 1 + NC - 1)

    @pl.when(is_panel)
    def _():
        @pl.loop(0, LEAD)
        def _(d):
            @pl.when(d != r)
            def _():
                se_copy(d).start()

    @pl.loop(0, SLOTS)
    def _(slot):
        block = children[tbl[slot]]
        stage0[slot] = jnp.where(swap, block[:, BLK:], block[:, :BLK])

    send_part(0)
    for t in range(2 * SUB):
        ins[t][SLOTS] = jnp.zeros((PART, BLK), F32)

    @pl.when(jnp.logical_not(is_panel))
    def _():
        send_part(1)

    xmat[...] = jnp.zeros_like(xmat)
    load_front.wait()

    def s_copy(i):
        at = pl.ds(pl.multiple_of(r * BLK, BLK), BLK)
        return pltpu.make_async_remote_copy(
            src_ref=panel.at[c, at],
            dst_ref=panel.at[c, at],
            send_sem=s_send.at[i],
            recv_sem=s_recv.at[r],
            device_id={"row": (r + i) % NR},
            device_id_type=MESH,
        )

    def s_wait(source):
        at = pl.ds(pl.multiple_of(source * BLK, BLK), BLK)
        pltpu.make_async_remote_copy(
            src_ref=panel.at[c, at],
            dst_ref=panel.at[c, at],
            send_sem=s_send.at[0],
            recv_sem=s_recv.at[source],
            device_id={"row": r},
            device_id_type=MESH,
        ).wait_recv()

    @pl.when(is_panel & is_lead)
    def _():
        in_s[r] = stage_s[r]

        @pl.loop(0, NR)
        def _(source):
            @pl.when(source != r)
            def _():
                se_wait(source)

        total = acc[0, :, :BLK]
        for source in range(NR):
            total = total + in_s[source]
        panel[c, pl.ds(pl.multiple_of(r * BLK, BLK), BLK), :] = total

        @pl.loop(1, NR)
        def _(i):
            s_copy(i).start()

    @pl.loop(0, SLOTS)
    def _(slot):
        block = children[tbl[slot]]
        stage1[slot] = jnp.where(swap, block[:, :BLK], block[:, BLK:])

    @pl.when(is_panel)
    def _():
        send_part(1)

        @pl.loop(0, LEAD)
        def _(source):
            @pl.when(source != r)
            def _():
                s_wait(source)

    def bc_copy(s, i, d, to):
        at = pl.ds(pl.multiple_of(i * BLK, BLK), BLK)
        return pltpu.make_async_remote_copy(
            src_ref=panel.at[s, at],
            dst_ref=panel.at[s, at],
            send_sem=bc_send.at[(s * 4 + d) * NCH + i],
            recv_sem=bc_recv.at[s * NCH + i],
            device_id={"col": to},
            device_id_type=MESH,
        )

    def targets(g, i):
        yp = y if g == 0 else (5 - y) % 4
        even = i % 2 == 0
        odd = i % 2 == 1
        up, down = (yp + 1) % 4, (yp + 3) % 4
        y_up = up if g == 0 else (5 - up) % 4
        y_down = down if g == 0 else (5 - down) % 4
        here, there = x_hi == 0, x_hi == 1
        return (
            (
                (here & (yp == 0)) | (there & ((even & (yp == 0)) | (odd & (yp == 3)))),
                x_hi * 8 + y_up * 2 + core,
            ),
            (
                (yp == 3) | ((yp == 0) & (here | even)) | (there & odd & (yp == 2)),
                x_hi * 8 + y_down * 2 + core,
            ),
            (
                here & ((even & (yp == 0)) | (odd & (yp == 3))),
                8 + y * 2 + core,
            ),
            (core >= 0, x_hi * 8 + y * 2 + 1 - core),
        )

    def sent(g, i):
        for d, (when, to) in enumerate(targets(g, i)):

            @pl.when(when)
            def _():
                bc_copy(2 * g + core, i, d, to).wait_send()

    def forward(step):
        odd = step % 2
        for g in range(2):
            s = 2 * g + core
            yp = y if g == 0 else (5 - y) % 4
            near = jnp.where(yp == 0, 0, jnp.where(yp == 2, 2, 1))
            far_odd = jnp.where(yp == 3, 2, jnp.where(yp == 1, 4, 3))
            far = jnp.where(odd == 1, far_odd, near + 1)
            i = step - LAG * jnp.where(x_hi == 0, near, far)

            @pl.when((i >= 0) & (i < NCH))
            def _():
                @pl.when(c != s)
                def _():
                    bc_copy(s, i, 0, c).wait_recv()

                @pl.when((c == s) & (i >= WINDOW))
                def _():
                    sent(g, i - WINDOW)

                for d, (when, to) in enumerate(targets(g, i)):

                    @pl.when(when)
                    def _():
                        bc_copy(s, i, d, to).start()

    def from_sibling(i):
        for g in range(2):
            s = 2 * g + 1 - core
            bc_copy(s, i, 0, c).wait_recv()

    def forward_all(first, last):
        @pl.loop(first, last)
        def _(step):
            forward(step)

    def assemble(t, store):
        q, part = t // SUB, pl.ds(t % SUB * PART, PART)

        @pl.loop(0, KR)
        def _(k):
            total = (
                acc[k, part, q * BLK : (q + 1) * BLK]
                + ins[t][tbl[SLOTS + k]]
                + ins[t][tbl[SLOTS + KR + k]]
            )
            store(k, total)

    def assemble_here(t):
        q, part = t // SUB, pl.ds(t % SUB * PART, PART)

        def store(k, total):
            acc[k, part, q * BLK : (q + 1) * BLK] = total

        assemble(t, store)

    def phase(t):
        if t < 2:
            send_part(t + 2)
        got_part(t)

        def store(k, total):
            at = pl.ds(pl.multiple_of(PANEL + t * SPAN + k * PART, PART), PART)
            panel[c, at, :] = total

        @pl.when(is_panel)
        def _():
            assemble(t, store)

        @pl.when(jnp.logical_not(is_panel))
        def _():
            assemble_here(t)

    other = r + 1 - 2 * (r % 2)
    is_relay = other == c % NR

    def p_rows(k, t):
        return pl.ds(pl.multiple_of(PANEL + t * SPAN + (x_hi + 2 * k) * PART, PART), PART)

    def p_copy(i, k, t, relayed=False):
        to = jnp.where(i < 4, r, other)
        to = jnp.where(i == 0, other, (to + 2 * (i % 4)) % NR)
        part = pl.ds(t * PART, PART)
        return pltpu.make_async_remote_copy(
            src_ref=psbuf.at[k, :, part] if relayed else panel.at[:, p_rows(k, t)],
            dst_ref=psbuf.at[k, :, part],
            send_sem=p_send.at[(t * 2 + k) * NR + i],
            recv_sem=p_recv.at[t * 2 + k],
            device_id={"row": to},
            device_id_type=MESH,
        )

    def p_each(t, act):
        @pl.when(is_root)
        def _():
            @pl.loop(0, 4)
            def _(i):
                for k in range(2):
                    act(p_copy(i, k, t))

            if t == SUB - 1:

                @pl.loop(5, 8)
                def _(i):
                    for k in range(2):
                        act(p_copy(i, k, t))

    def p_relay(t, act):
        @pl.loop(1, 4)
        def _(i):
            for k in range(2):
                act(p_copy(i, k, t, True))

    def send_rows(t):
        from_sibling(LEAD + t * TURN)
        p_each(t, lambda copy: copy.start())

        @pl.when(is_root)
        def _():
            for k in range(2):
                psbuf[k, :, t * PART : (t + 1) * PART, :] = panel[:, p_rows(k, t), :]

        if t > 0:

            @pl.when(is_relay)
            def _():
                for k in range(2):
                    p_copy(0, k, t - 1).wait_recv()
                p_relay(t - 1, lambda copy: copy.start())

    forward_all(0, LEAD)
    phase(0)
    forward_all(LEAD, LEAD + TURN)
    phase(1)
    forward_all(LEAD + TURN, LEAD + TURN + TURN // 2)
    send_part(SUB)
    forward_all(LEAD + TURN + TURN // 2, AHEAD)
    for i in range(LEAD):
        from_sibling(i)

    send_rows(0)
    for i in range(4):
        for j in range(4):
            rows = slice(i * BLK, (i + 1) * BLK)
            cols = slice(j * BLK, (j + 1) * BLK)
            smat[rows, cols] = 0.5 * (panel[j, rows, :] + panel[i, cols, :].T)

    @pl.loop(0, 4)
    def _(b):
        for t in range(2, SUB):

            @pl.when(b == t - 2)
            def _():
                phase(t)

        at = pl.ds(pl.multiple_of(b * BLK, BLK), BLK)
        block[...] = smat[at, at]
        for k in range(1, 4):

            @pl.when(b == k)
            def _():
                x = xmat[: k * BLK, : k * BLK]
                lb = nt(smat[k * BLK : (k + 1) * BLK, : k * BLK], x, HI)
                block[...] -= nt(lb, lb, HI)
                lbx[:, : k * BLK] = nn(lb, x, HI)

        def between(n):
            first = AHEAD + 8 * b + 2 * n
            forward_all(first, first + 2)
            for t, point in enumerate((SEND_5, SEND_6, SEND_7)):

                @pl.when(4 * b + n == point)
                def _():
                    send_part(SUB + 1 + t)

            for t in range(1, SUB):
                due = LEAD + t * TURN + 4 * LAG - AHEAD - 1
                due = -(-due // 2)

                @pl.when(4 * b + n == due)
                def _():
                    send_rows(t)

        v = inverse_of_factor(block[...], between)
        for k in range(1, 4):

            @pl.when(b == k)
            def _():
                xmat[k * BLK : (k + 1) * BLK, : k * BLK] = -nn(v, lbx[:, : k * BLK], HI)

        xmat[at, at] = v

    last = AHEAD + 32
    forward_all(last, last + 2)

    for t in range(SUB):

        @pl.when(jnp.logical_not(is_root | (is_relay & (t < SUB - 1))))
        def _():
            for k in range(2):
                p_copy(0, k, t).wait_recv()

    x_high, x_low = split(xmat[...])

    def three(product, a, high, low):
        a_high, a_low = split(a)
        return product(a_high, high) + (product(a_high, low) + product(a_low, high))

    for k in range(2):
        ps = jnp.concatenate([psbuf[k, s] for s in range(4)], axis=1)
        wt = three(nn, three(nt, ps, x_high, x_low), x_high, x_low)
        if k == 0:
            at = pl.ds(pl.multiple_of((c % 4) * BLK, BLK), BLK)
            wt = jnp.where(is_panel, -xmat[at, :], wt)
        high, low = split(wt)
        wth[k * BLK : (k + 1) * BLK, :] = high
        wtl[k * BLK : (k + 1) * BLK, :] = low

    forward_all(last + 2, last + 3)

    drop = is_panel & (lax.broadcasted_iota(jnp.int32, (1, 2 * BLK), 1) < BLK)

    def out_copy(t, u):
        return pltpu.make_async_copy(
            acc.at[pl.ds(u * UNIT, UNIT), pl.ds(t * PART, PART)],
            out.at[pl.ds(u * UNIT, UNIT), pl.ds(t * PART, PART)],
            out_sem.at[t * 4 + u],
        )

    def update(t):
        @pl.loop(1, TURN)
        def _(i):
            from_sibling(LEAD + t * TURN + i)

        @pl.loop(0, KR // UNIT)
        def _(u):
            first = pl.multiple_of(PANEL + t * SPAN + u * UNIT * PART, PART)
            rows = jnp.concatenate(
                [panel[s, pl.ds(first, UNIT * PART), :] for s in range(4)], axis=1
            )
            lead_at = pl.ds(pl.multiple_of((r % 4) * BLK + t * PART, PART), PART)
            head = jnp.where(is_lead & (u == 0), smat[lead_at, :], rows[:PART])
            rows = jnp.concatenate([head, rows[PART:]], axis=0)
            high, low = split(rows)
            total = nt(high, wth[...]) + (nt(high, wtl[...]) + nt(low, wth[...]))
            for b in range(UNIT):
                at = u * UNIT + b
                part = slice(t * PART, (t + 1) * PART)
                acc[at, part, :] = (
                    jnp.where(drop, 0.0, acc[at, part, :]) - total[b * PART : (b + 1) * PART]
                )

    update(0)
    forward_all(last + 3, last + 5)
    update(1)
    forward_all(last + 5, STEPS)
    update(2)
    update(3)

    for t in range(SUB):
        got_part(SUB + t)
        assemble_here(SUB + t)

        @pl.loop(0, KR // UNIT)
        def _(u):
            out_copy(t, u).start()

    for t in range(SUB):

        @pl.loop(0, KR // UNIT)
        def _(u):
            out_copy(t, u).wait()

        sent_part(t)
        sent_part(SUB + t)

    @pl.when(is_panel)
    def _():
        @pl.loop(0, LEAD)
        def _(d):
            @pl.when(d != r)
            def _():
                se_copy(d).wait_send()

    @pl.when(is_panel & is_lead)
    def _():
        @pl.loop(1, NR)
        def _(i):
            s_copy(i).wait_send()

    for t in range(SUB):
        p_each(t, lambda copy: copy.wait_send())
        if t < SUB - 1:

            @pl.when(is_relay)
            def _():
                p_relay(t, lambda copy: copy.wait_send())

    for g in range(2):

        @pl.loop(0, NCH)
        def _(i):
            @pl.when((c != 2 * g + core) | (i >= NCH - WINDOW))
            def _():
                sent(g, i)


def tables(row_map, col_map):
    my_row = lax.axis_index("row")
    my_col = lax.axis_index("col")
    layout = row_map.reshape(NR, -1)
    count = layout.shape[1]
    owner = layout % NR
    counter = jnp.arange(count)
    earlier = (owner[:, :, None] == owner[:, None, :]) & (
        counter[None, None, :] < counter[None, :, None]
    )
    rank = jnp.sum(earlier.astype(jnp.int32), axis=2)
    slot_out = owner * MOST + rank
    mine = lax.dynamic_index_in_dim(slot_out, my_row, 0, keepdims=False)
    send = jnp.sum(
        jnp.where(mine[None, :] == jnp.arange(SLOTS)[:, None], counter[None, :], 0), axis=1
    )
    slot_in = (jnp.arange(NR)[:, None] * MOST + rank).reshape(2, -1)
    wanted = jnp.arange(KR) * NR + my_row
    hit = layout.reshape(2, 1, -1) == wanted[None, :, None]
    receive = SLOTS + jnp.sum(jnp.where(hit, slot_in[:, None, :] - SLOTS, 0), axis=2)
    child = my_row // (NR // 2)
    first = lax.dynamic_index_in_dim(
        col_map.reshape(2, NC, 2)[:, :, 0].reshape(-1), child * NC + my_col, 0
    )
    own = lax.dynamic_index_in_dim(layout, my_row, 0, keepdims=False)
    lead = jnp.sum(
        jnp.where(own[None, :] == jnp.arange(LEAD)[:, None], counter[None, :] + 1, 0), axis=1
    )
    return jnp.concatenate([send, receive.reshape(-1), first // NC, lead]).astype(jnp.int32)


def local(front, children, row_map, col_map):
    table = tables(row_map, col_map)
    hbm = pl.BlockSpec(memory_space=pl.ANY)
    blocks = children.reshape(-1, BLK, 2 * BLK)
    tile = (BLK, BLK)
    held = front.reshape(KR, BLK, 2 * BLK)
    vmem = lambda *shape: pltpu.VMEM(shape, F32)
    dma = lambda count: pltpu.SemaphoreType.DMA((count,))
    result = pl.pallas_call(
        kernel,
        out_shape=jax.ShapeDtypeStruct(held.shape, F32),
        in_specs=[pl.BlockSpec(memory_space=pltpu.SMEM), hbm, hbm],
        out_specs=hbm,
        scratch_shapes=[
            vmem(*blocks.shape),
            vmem(*held.shape),
            vmem(SLOTS, *tile),
            vmem(SLOTS, *tile),
            *[vmem(SLOTS + 1, PART, BLK) for _ in range(2 * SUB)],
            vmem(LEAD, *tile),
            vmem(NR, *tile),
            vmem(4, NCH * BLK, BLK),
            vmem(2, 4, *tile),
            vmem(PANEL, PANEL),
            vmem(PANEL, PANEL),
            vmem(*tile),
            vmem(BLK, PANEL),
            pltpu.VMEM((2 * BLK, PANEL), BF16),
            pltpu.VMEM((2 * BLK, PANEL), BF16),
            dma(2),
            dma(2 * SUB * NR),
            dma(2 * SUB * NR),
            dma(2 * SUB),
            dma(16 * NCH),
            dma(4 * NCH),
            dma(LEAD),
            dma(NR),
            dma(NR),
            dma(LEAD),
            dma(2 * SUB * NR),
            dma(2 * SUB),
            dma(16),
        ],
        compiler_params=pltpu.CompilerParams(
            collective_id=0, has_side_effects=True, vmem_limit_bytes=60 * 2**20
        ),
    )(table, held, blocks)
    return result.reshape(front.shape)


def solution(mesh):
    placed = (P("row", "col"), P("row", "col"), P(), P())
    return jax.shard_map(
        local, mesh=mesh, in_specs=placed, out_specs=P("row", "col"), check_vma=False
    )
```

```python
import jax
import jax.numpy as jnp
from jax import lax
from jax.experimental import pallas as pl
from jax.experimental.pallas import tpu as pltpu
from jax.sharding import PartitionSpec as P

BLK = 128
PANEL = 512
NR = 8
NC = 16
MOST = 8
SLOTS = NR * MOST
KR = 44
SUB = 4
PART = BLK // SUB
SPAN = KR * PART
NCH = (PANEL + KR * BLK) // BLK
LEAD = PANEL // BLK
TURN = SPAN // BLK
UNIT = 11
WINDOW = 6
LAG = 4
SEND_5 = 3
SEND_6 = 7
SEND_7 = 11
STEPS = NCH + 4 * LAG
AHEAD = LEAD + 2 * TURN
HI = lax.Precision.HIGHEST
MESH = pl.DeviceIdType.MESH
F32 = jnp.float32
BF16 = jnp.bfloat16


def nt(a, b, precision=None):
    return lax.dot_general(
        a, b, (((1,), (1,)), ((), ())), precision=precision, preferred_element_type=F32
    )


def nn(a, b, precision=None):
    return lax.dot_general(
        a, b, (((1,), (0,)), ((), ())), precision=precision, preferred_element_type=F32
    )


def split(x):
    high = x.astype(BF16)
    return high, (x - high.astype(F32)).astype(BF16)


def inverse_of_factor(a, between):
    rows = lax.broadcasted_iota(jnp.int32, (BLK, 1), 0)
    eye = rows == lax.broadcasted_iota(jnp.int32, (BLK, BLK), 1)
    e = eye.astype(F32)
    done_a, done_e = [], []
    for first in range(0, BLK, 32):
        below = rows[first:]
        for j in range(first, first + 32):
            i = j - first
            pivot = 1.0 / a[i : i + 1, j : j + 1]
            col = jnp.where(below > j, a[:, j : j + 1], 0.0)
            row_a = a[i : i + 1, :] * pivot
            row_e = e[i : i + 1, :] * pivot
            a = a - col * row_a
            e = e - col * row_e
        done_a.append(a[:32])
        done_e.append(e[:32])
        a, e = a[32:], e[32:]
        between(first // 32)
    a = jnp.concatenate(done_a, axis=0)
    e = jnp.concatenate(done_e, axis=0)
    d = jnp.sum(jnp.where(eye, a, 0.0), axis=1, keepdims=True)
    s = lax.rsqrt(d)
    s = s * (1.5 - 0.5 * d * s * s)
    return e * s


def kernel(
    tbl, front, children_hbm, out,
    children, acc, stage0, stage1, in00, in01, in02, in03, in10, in11, in12, in13, stage_s, in_s, panel, psbuf, smat, xmat, block, lbx, wth, wtl,
    load_sem, ex_send, ex_recv, own_sem, bc_send, bc_recv, se_send, se_recv, s_send, s_recv, p_send, p_recv, out_sem,
):
    r = lax.axis_index("row")
    c = lax.axis_index("col")
    x_hi = c // 8
    y = (c // 2) % 4
    core = c % 2
    is_panel = c < 4
    is_lead = r < 4
    is_root = r == c % NR
    ins = (in00, in01, in02, in03, in10, in11, in12, in13)

    load_children = pltpu.make_async_copy(children_hbm, children, load_sem.at[0])
    load_front = pltpu.make_async_copy(front, acc, load_sem.at[1])
    load_children.start()
    load_front.start()

    barrier = pltpu.get_barrier_semaphore()

    @pl.loop(1, NR)
    def _(i):
        pl.semaphore_signal(barrier, inc=1, device_id={"row": (r + i) % NR}, device_id_type=MESH)

    @pl.loop(1, NC)
    def _(i):
        pl.semaphore_signal(barrier, inc=1, device_id={"col": (c + i) % NC}, device_id_type=MESH)

    swap = tbl[SLOTS + 2 * KR] == 1

    def ex_parts(t, slots):
        at = pl.ds(t % SUB * PART, PART)
        return (stage0 if t < SUB else stage1).at[slots, at]

    def ex_copy(t, i):
        to = (r + i) % NR
        return pltpu.make_async_remote_copy(
            src_ref=ex_parts(t, pl.ds(to * MOST, MOST)),
            dst_ref=ins[t].at[pl.ds(r * MOST, MOST)],
            send_sem=ex_send.at[t * NR + i],
            recv_sem=ex_recv.at[t * NR + i],
            device_id={"row": to},
            device_id_type=MESH,
        )

    def own_copy(t):
        mine = pl.ds(r * MOST, MOST)
        return pltpu.make_async_copy(ex_parts(t, mine), ins[t].at[mine], own_sem.at[t])

    def send_part(t):
        own_copy(t).start()

        @pl.loop(1, NR)
        def _(i):
            ex_copy(t, i).start()

    def sent_part(t):
        @pl.loop(1, NR)
        def _(i):
            ex_copy(t, i).wait_send()

    def send_later(t):
        @pl.when(is_panel)
        def _():
            send_part(t)

        if t + 1 < 2 * SUB:

            @pl.when(jnp.logical_not(is_panel))
            def _():
                send_part(t + 1)

    def got_part(t):
        own_copy(t).wait()

        @pl.loop(1, NR)
        def _(i):
            ex_copy(t, i).wait_recv()

    def se_copy(d):
        return pltpu.make_async_remote_copy(
            src_ref=stage_s.at[d],
            dst_ref=in_s.at[r],
            send_sem=se_send.at[d],
            recv_sem=se_recv.at[r],
            device_id={"row": d},
            device_id_type=MESH,
        )

    def se_wait(source):
        pltpu.make_async_remote_copy(
            src_ref=stage_s.at[0],
            dst_ref=in_s.at[source],
            send_sem=se_send.at[0],
            recv_sem=se_recv.at[source],
            device_id={"row": r},
            device_id_type=MESH,
        ).wait_recv()

    load_children.wait()

    @pl.loop(0, LEAD)
    def _(d):
        found = tbl[SLOTS + 2 * KR + 1 + d]
        block = children[jnp.maximum(found - 1, 0)]
        half = jnp.where(swap, block[:, BLK:], block[:, :BLK])
        stage_s[d] = jnp.where(found > 0, half, 0.0)

    pl.semaphore_wait(barrier, NR - 1 + NC - 1)

    @pl.when(is_panel)
    def _():
        @pl.loop(0, LEAD)
        def _(d):
            @pl.when(d != r)
            def _():
                se_copy(d).start()

    @pl.loop(0, SLOTS)
    def _(slot):
        block = children[tbl[slot]]
        stage0[slot] = jnp.where(swap, block[:, BLK:], block[:, :BLK])

    send_part(0)
    for t in range(2 * SUB):
        ins[t][SLOTS] = jnp.zeros((PART, BLK), F32)

    @pl.when(jnp.logical_not(is_panel))
    def _():
        send_part(1)
        send_part(2)

    xmat[...] = jnp.zeros_like(xmat)
    load_front.wait()

    def s_copy(i):
        at = pl.ds(pl.multiple_of(r * BLK, BLK), BLK)
        return pltpu.make_async_remote_copy(
            src_ref=panel.at[c, at],
            dst_ref=panel.at[c, at],
            send_sem=s_send.at[i],
            recv_sem=s_recv.at[r],
            device_id={"row": (r + i) % NR},
            device_id_type=MESH,
        )

    def s_wait(source):
        at = pl.ds(pl.multiple_of(source * BLK, BLK), BLK)
        pltpu.make_async_remote_copy(
            src_ref=panel.at[c, at],
            dst_ref=panel.at[c, at],
            send_sem=s_send.at[0],
            recv_sem=s_recv.at[source],
            device_id={"row": r},
            device_id_type=MESH,
        ).wait_recv()

    @pl.when(is_panel & is_lead)
    def _():
        in_s[r] = stage_s[r]

        @pl.loop(0, NR)
        def _(source):
            @pl.when(source != r)
            def _():
                se_wait(source)

        total = acc[0, :, :BLK]
        for source in range(NR):
            total = total + in_s[source]
        panel[c, pl.ds(pl.multiple_of(r * BLK, BLK), BLK), :] = total

        @pl.loop(1, NR)
        def _(i):
            s_copy(i).start()

    @pl.loop(0, SLOTS)
    def _(slot):
        block = children[tbl[slot]]
        stage1[slot] = jnp.where(swap, block[:, :BLK], block[:, BLK:])

    @pl.when(is_panel)
    def _():
        send_part(1)

        @pl.loop(0, LEAD)
        def _(source):
            @pl.when(source != r)
            def _():
                s_wait(source)

    def bc_copy(s, i, d, to):
        at = pl.ds(pl.multiple_of(i * BLK, BLK), BLK)
        return pltpu.make_async_remote_copy(
            src_ref=panel.at[s, at],
            dst_ref=panel.at[s, at],
            send_sem=bc_send.at[(s * 4 + d) * NCH + i],
            recv_sem=bc_recv.at[s * NCH + i],
            device_id={"col": to},
            device_id_type=MESH,
        )

    def targets(g, i):
        yp = y if g == 0 else (5 - y) % 4
        even = i % 2 == 0
        odd = i % 2 == 1
        up, down = (yp + 1) % 4, (yp + 3) % 4
        y_up = up if g == 0 else (5 - up) % 4
        y_down = down if g == 0 else (5 - down) % 4
        here, there = x_hi == 0, x_hi == 1
        return (
            (
                (here & (yp == 0)) | (there & ((even & (yp == 0)) | (odd & (yp == 3)))),
                x_hi * 8 + y_up * 2 + core,
            ),
            (
                (yp == 3) | ((yp == 0) & (here | even)) | (there & odd & (yp == 2)),
                x_hi * 8 + y_down * 2 + core,
            ),
            (
                here & ((even & (yp == 0)) | (odd & (yp == 3))),
                8 + y * 2 + core,
            ),
            (core >= 0, x_hi * 8 + y * 2 + 1 - core),
        )

    def sent(g, i):
        for d, (when, to) in enumerate(targets(g, i)):

            @pl.when(when)
            def _():
                bc_copy(2 * g + core, i, d, to).wait_send()

    def forward(step):
        odd = step % 2
        for g in range(2):
            s = 2 * g + core
            yp = y if g == 0 else (5 - y) % 4
            near = jnp.where(yp == 0, 0, jnp.where(yp == 2, 2, 1))
            far_odd = jnp.where(yp == 3, 2, jnp.where(yp == 1, 4, 3))
            far = jnp.where(odd == 1, far_odd, near + 1)
            i = step - LAG * jnp.where(x_hi == 0, near, far)

            @pl.when((i >= 0) & (i < NCH))
            def _():
                @pl.when(c != s)
                def _():
                    bc_copy(s, i, 0, c).wait_recv()

                @pl.when((c == s) & (i >= WINDOW))
                def _():
                    sent(g, i - WINDOW)

                for d, (when, to) in enumerate(targets(g, i)):

                    @pl.when(when)
                    def _():
                        bc_copy(s, i, d, to).start()

    def from_sibling(i):
        for g in range(2):
            s = 2 * g + 1 - core
            bc_copy(s, i, 0, c).wait_recv()

    def forward_all(first, last):
        @pl.loop(first, last)
        def _(step):
            forward(step)

    def assemble(t, store):
        q, part = t // SUB, pl.ds(t % SUB * PART, PART)

        @pl.loop(0, KR)
        def _(k):
            total = (
                acc[k, part, q * BLK : (q + 1) * BLK]
                + ins[t][tbl[SLOTS + k]]
                + ins[t][tbl[SLOTS + KR + k]]
            )
            store(k, total)

    def assemble_here(t):
        q, part = t // SUB, pl.ds(t % SUB * PART, PART)

        def store(k, total):
            acc[k, part, q * BLK : (q + 1) * BLK] = total

        assemble(t, store)

    def phase(t):
        if t < 2:
            send_later(t + 2)
        got_part(t)

        def store(k, total):
            at = pl.ds(pl.multiple_of(PANEL + t * SPAN + k * PART, PART), PART)
            panel[c, at, :] = total

        @pl.when(is_panel)
        def _():
            assemble(t, store)

        @pl.when(jnp.logical_not(is_panel))
        def _():
            assemble_here(t)

    other = r + 1 - 2 * (r % 2)
    is_relay = other == c % NR

    def p_rows(k, t):
        return pl.ds(pl.multiple_of(PANEL + t * SPAN + (x_hi + 2 * k) * PART, PART), PART)

    def p_copy(i, k, t, relayed=False):
        to = jnp.where(i < 4, r, other)
        to = jnp.where(i == 0, other, (to + 2 * (i % 4)) % NR)
        part = pl.ds(t * PART, PART)
        return pltpu.make_async_remote_copy(
            src_ref=psbuf.at[k, :, part] if relayed else panel.at[:, p_rows(k, t)],
            dst_ref=psbuf.at[k, :, part],
            send_sem=p_send.at[(t * 2 + k) * NR + i],
            recv_sem=p_recv.at[t * 2 + k],
            device_id={"row": to},
            device_id_type=MESH,
        )

    def p_each(t, act):
        @pl.when(is_root)
        def _():
            @pl.loop(0, 4)
            def _(i):
                for k in range(2):
                    act(p_copy(i, k, t))

            if t == SUB - 1:

                @pl.loop(5, 8)
                def _(i):
                    for k in range(2):
                        act(p_copy(i, k, t))

    def p_relay(t, act):
        @pl.loop(1, 4)
        def _(i):
            for k in range(2):
                act(p_copy(i, k, t, True))

    def send_rows(t):
        from_sibling(LEAD + t * TURN)
        p_each(t, lambda copy: copy.start())

        @pl.when(is_root)
        def _():
            for k in range(2):
                psbuf[k, :, t * PART : (t + 1) * PART, :] = panel[:, p_rows(k, t), :]

        if t > 0:

            @pl.when(is_relay)
            def _():
                for k in range(2):
                    p_copy(0, k, t - 1).wait_recv()
                p_relay(t - 1, lambda copy: copy.start())

    forward_all(0, LEAD)
    phase(0)
    forward_all(LEAD, LEAD + TURN)
    phase(1)
    forward_all(LEAD + TURN, LEAD + TURN + TURN // 2)
    send_later(SUB)
    forward_all(LEAD + TURN + TURN // 2, AHEAD)
    for i in range(LEAD):
        from_sibling(i)

    send_rows(0)
    for i in range(4):
        for j in range(4):
            rows = slice(i * BLK, (i + 1) * BLK)
            cols = slice(j * BLK, (j + 1) * BLK)
            smat[rows, cols] = 0.5 * (panel[j, rows, :] + panel[i, cols, :].T)

    @pl.loop(0, 4)
    def _(b):
        for t in range(2, SUB):

            @pl.when(b == t - 2)
            def _():
                phase(t)

        at = pl.ds(pl.multiple_of(b * BLK, BLK), BLK)
        block[...] = smat[at, at]
        for k in range(1, 4):

            @pl.when(b == k)
            def _():
                x = xmat[: k * BLK, : k * BLK]
                lb = nt(smat[k * BLK : (k + 1) * BLK, : k * BLK], x, HI)
                block[...] -= nt(lb, lb, HI)
                lbx[:, : k * BLK] = nn(lb, x, HI)

        def between(n):
            first = AHEAD + 8 * b + 2 * n
            forward_all(first, first + 2)
            for t, point in enumerate((SEND_5, SEND_6, SEND_7)):

                @pl.when(4 * b + n == point)
                def _():
                    send_later(SUB + 1 + t)

            for t in range(1, SUB):
                due = LEAD + t * TURN + 4 * LAG - AHEAD - 1
                due = -(-due // 2)

                @pl.when(4 * b + n == due)
                def _():
                    send_rows(t)

        v = inverse_of_factor(block[...], between)
        for k in range(1, 4):

            @pl.when(b == k)
            def _():
                xmat[k * BLK : (k + 1) * BLK, : k * BLK] = -nn(v, lbx[:, : k * BLK], HI)

        xmat[at, at] = v

    last = AHEAD + 32
    forward_all(last, last + 2)

    for t in range(SUB):

        @pl.when(jnp.logical_not(is_root | (is_relay & (t < SUB - 1))))
        def _():
            for k in range(2):
                p_copy(0, k, t).wait_recv()

    x_high, x_low = split(xmat[...])

    def three(product, a, high, low):
        a_high, a_low = split(a)
        return product(a_high, high) + (product(a_high, low) + product(a_low, high))

    for k in range(2):
        ps = jnp.concatenate([psbuf[k, s] for s in range(4)], axis=1)
        wt = three(nn, three(nt, ps, x_high, x_low), x_high, x_low)
        if k == 0:
            at = pl.ds(pl.multiple_of((c % 4) * BLK, BLK), BLK)
            wt = jnp.where(is_panel, -xmat[at, :], wt)
        high, low = split(wt)
        wth[k * BLK : (k + 1) * BLK, :] = high
        wtl[k * BLK : (k + 1) * BLK, :] = low

    forward_all(last + 2, last + 3)

    drop = is_panel & (lax.broadcasted_iota(jnp.int32, (1, 2 * BLK), 1) < BLK)

    def out_copy(t, u):
        return pltpu.make_async_copy(
            acc.at[pl.ds(u * UNIT, UNIT), pl.ds(t * PART, PART)],
            out.at[pl.ds(u * UNIT, UNIT), pl.ds(t * PART, PART)],
            out_sem.at[t * 4 + u],
        )

    def update(t):
        @pl.loop(1, TURN)
        def _(i):
            from_sibling(LEAD + t * TURN + i)

        @pl.loop(0, KR // UNIT)
        def _(u):
            first = pl.multiple_of(PANEL + t * SPAN + u * UNIT * PART, PART)
            rows = jnp.concatenate(
                [panel[s, pl.ds(first, UNIT * PART), :] for s in range(4)], axis=1
            )
            lead_at = pl.ds(pl.multiple_of((r % 4) * BLK + t * PART, PART), PART)
            head = jnp.where(is_lead & (u == 0), smat[lead_at, :], rows[:PART])
            rows = jnp.concatenate([head, rows[PART:]], axis=0)
            high, low = split(rows)
            total = nt(high, wth[...]) + (nt(high, wtl[...]) + nt(low, wth[...]))
            for b in range(UNIT):
                at = u * UNIT + b
                part = slice(t * PART, (t + 1) * PART)
                acc[at, part, :] = (
                    jnp.where(drop, 0.0, acc[at, part, :]) - total[b * PART : (b + 1) * PART]
                )

    update(0)
    forward_all(last + 3, last + 5)
    update(1)
    forward_all(last + 5, STEPS)
    update(2)
    update(3)

    for t in range(SUB):
        got_part(SUB + t)
        assemble_here(SUB + t)

        @pl.loop(0, KR // UNIT)
        def _(u):
            out_copy(t, u).start()

    for t in range(SUB):

        @pl.loop(0, KR // UNIT)
        def _(u):
            out_copy(t, u).wait()

        sent_part(t)
        sent_part(SUB + t)

    @pl.when(is_panel)
    def _():
        @pl.loop(0, LEAD)
        def _(d):
            @pl.when(d != r)
            def _():
                se_copy(d).wait_send()

    @pl.when(is_panel & is_lead)
    def _():
        @pl.loop(1, NR)
        def _(i):
            s_copy(i).wait_send()

    for t in range(SUB):
        p_each(t, lambda copy: copy.wait_send())
        if t < SUB - 1:

            @pl.when(is_relay)
            def _():
                p_relay(t, lambda copy: copy.wait_send())

    for g in range(2):

        @pl.loop(0, NCH)
        def _(i):
            @pl.when((c != 2 * g + core) | (i >= NCH - WINDOW))
            def _():
                sent(g, i)


def tables(row_map, col_map):
    my_row = lax.axis_index("row")
    my_col = lax.axis_index("col")
    layout = row_map.reshape(NR, -1)
    count = layout.shape[1]
    owner = layout % NR
    counter = jnp.arange(count)
    earlier = (owner[:, :, None] == owner[:, None, :]) & (
        counter[None, None, :] < counter[None, :, None]
    )
    rank = jnp.sum(earlier.astype(jnp.int32), axis=2)
    slot_out = owner * MOST + rank
    mine = lax.dynamic_index_in_dim(slot_out, my_row, 0, keepdims=False)
    send = jnp.sum(
        jnp.where(mine[None, :] == jnp.arange(SLOTS)[:, None], counter[None, :], 0), axis=1
    )
    slot_in = (jnp.arange(NR)[:, None] * MOST + rank).reshape(2, -1)
    wanted = jnp.arange(KR) * NR + my_row
    hit = layout.reshape(2, 1, -1) == wanted[None, :, None]
    receive = SLOTS + jnp.sum(jnp.where(hit, slot_in[:, None, :] - SLOTS, 0), axis=2)
    child = my_row // (NR // 2)
    first = lax.dynamic_index_in_dim(
        col_map.reshape(2, NC, 2)[:, :, 0].reshape(-1), child * NC + my_col, 0
    )
    own = lax.dynamic_index_in_dim(layout, my_row, 0, keepdims=False)
    lead = jnp.sum(
        jnp.where(own[None, :] == jnp.arange(LEAD)[:, None], counter[None, :] + 1, 0), axis=1
    )
    return jnp.concatenate([send, receive.reshape(-1), first // NC, lead]).astype(jnp.int32)


def local(front, children, row_map, col_map):
    table = tables(row_map, col_map)
    hbm = pl.BlockSpec(memory_space=pl.ANY)
    blocks = children.reshape(-1, BLK, 2 * BLK)
    tile = (BLK, BLK)
    held = front.reshape(KR, BLK, 2 * BLK)
    vmem = lambda *shape: pltpu.VMEM(shape, F32)
    dma = lambda count: pltpu.SemaphoreType.DMA((count,))
    result = pl.pallas_call(
        kernel,
        out_shape=jax.ShapeDtypeStruct(held.shape, F32),
        in_specs=[pl.BlockSpec(memory_space=pltpu.SMEM), hbm, hbm],
        out_specs=hbm,
        scratch_shapes=[
            vmem(*blocks.shape),
            vmem(*held.shape),
            vmem(SLOTS, *tile),
            vmem(SLOTS, *tile),
            *[vmem(SLOTS + 1, PART, BLK) for _ in range(2 * SUB)],
            vmem(LEAD, *tile),
            vmem(NR, *tile),
            vmem(4, NCH * BLK, BLK),
            vmem(2, 4, *tile),
            vmem(PANEL, PANEL),
            vmem(PANEL, PANEL),
            vmem(*tile),
            vmem(BLK, PANEL),
            pltpu.VMEM((2 * BLK, PANEL), BF16),
            pltpu.VMEM((2 * BLK, PANEL), BF16),
            dma(2),
            dma(2 * SUB * NR),
            dma(2 * SUB * NR),
            dma(2 * SUB),
            dma(16 * NCH),
            dma(4 * NCH),
            dma(LEAD),
            dma(NR),
            dma(NR),
            dma(LEAD),
            dma(2 * SUB * NR),
            dma(2 * SUB),
            dma(16),
        ],
        compiler_params=pltpu.CompilerParams(
            collective_id=0, has_side_effects=True, vmem_limit_bytes=60 * 2**20
        ),
    )(table, held, blocks)
    return result.reshape(front.shape)


def solution(mesh):
    placed = (P("row", "col"), P("row", "col"), P(), P())
    return jax.shard_map(
        local, mesh=mesh, in_specs=placed, out_specs=P("row", "col"), check_vma=False
    )
```
